32 devices in a mesh: groups: 2 (over x), section: 16 (over z, y, core).
Axes of the slice: x: 2, y: 2, z: 4, core: 2. Of those that a mesh axis runs over, the one named last changes fastest.
Arguments:
- feats: bfloat16 [256, 24576], P('groups', 'section'), parts along dimension 0, may hold values from -6 to 6
- uniting_weight: bfloat16 [24576, 8192], P('section'), may hold values from -0.0546875 to 0.0546875
- embeds_verified: bfloat16 [256, 8192], P('groups', 'section'), parts along dimension 0, may hold values from -6 to 6
- draft_embeds: bfloat16 [4, 256, 8192], P(None, 'groups', 'section'), parts along dimension 1, may hold values from -6 to 6
- gain_embed: bfloat16 [8192], P('section'), may hold values from 0.25 to 1.75
- gain_hidden: bfloat16 [8192], P('section'), may hold values from 0.25 to 1.75
- proj_embed: bfloat16 [8192, 5120], P('section'), may hold values from -0.0625 to 0.0625
- proj_hidden: bfloat16 [8192, 5120], P('section'), may hold values from -0.0625 to 0.0625
- out_proj: bfloat16 [4096, 8192], P(None, 'section'), may hold values from -0.09375 to 0.09375
- lengths: int32 [32], P('groups'), parts along dimension 0, may hold values from 1 to 32, 128 in all
- root_seq: int32 [256], P('groups'), parts along dimension 0, may hold values from 0 to 15
- parents: int32 [3, 256], P(None, 'groups'), parts along dimension 1, may hold values from 0 to 127
Outputs:
- drafts: bfloat16 [1024, 8192], P(('groups', 'section')), parts along dimension 0
The draws below stay inside these ranges and needn't reach their ends.
There are 2 independent parts, one for each index of `groups`. The reference program is written for one: setup_inputs(seed, part) draws one part's arguments, and reference() takes and returns one part's arrays. A program takes and returns all parts, laid end to end along the dimension named above; an argument that names none is the same for every part. Nothing has to cross between parts.
Inputs may be any that keep to these rules, and one draw needn't show every extreme that they name: `lengths`: sum to 128; the largest is exactly 32.
All inputs are finite; a program needn't handle non-finite values.
Results may differ from the reference program's by a relative error of at most 0.012.
Values may be sent and summed in bfloat16 or wider, within the bound.
A program may use at most 128 MiB of HBM per device.

```python
import math
import jax
import jax.numpy as jnp
import numpy as np
from jax import lax

D = 8192
HD = 128
QH = 32
KVH = 4
STEPS = 4
ROWS = 128
SEQS = 16
NODES = 128


def plant(result, key, least, high):
    shape = result.shape
    spot = [jax.random.randint(jax.random.fold_in(key, axis), (), 0, shape[axis]) for axis in range(len(shape))]
    result = result.at[tuple(spot)].set(least)
    longest = shape.index(max(shape))
    spot[longest] = (spot[longest] + 1) % shape[longest]
    return result.at[tuple(spot)].set(high)


def with_spikes(entries, own_key, source, target, blocks, factor):
    owner, partner = [(jnp.arange(entries.shape[axis_at]) // (entries.shape[axis_at] // blocks)).reshape([-1 if axis == axis_at else 1 for axis in range(entries.ndim)]) for axis_at in (source, target)]
    chosen = jax.random.permutation(own_key, blocks)[partner]
    strong = (owner == chosen) | (owner == (partner + blocks // 2) % blocks)
    return jnp.where(strong, factor * entries, entries)


def level_of(stream_key, dims, shards, least, high):
    def one(axis_at, parts):
        heights = jax.random.uniform(jax.random.fold_in(jax.random.fold_in(stream_key, 6), axis_at), (parts,), jnp.float32, least / len(shards), high / len(shards))
        return jnp.repeat(jnp.exp(heights), dims[axis_at] // parts).reshape((-1,) + (1,) * (len(dims) - axis_at - 1))

    level = one(*shards[0])
    for cut in shards[1:]:
        level = level * one(*cut)
    return level


def split_up(amount, total, most, lean):
    weights = [(1 << 20) // math.isqrt(standing ** lean) + 1 for standing in range(2, amount + 1)]
    surplus, given = total - most - (amount - 1), [1] * (amount - 1)
    while surplus > 0:
        free = [i for i in range(amount - 1) if given[i] < most]
        mass, budget = sum([weights[i] for i in free]), surplus
        for i in free:
            more = min(most - given[i], max(1, budget * weights[i] // mass), surplus)
            given[i] = given[i] + more
            surplus = surplus - more
    return np.array([most] + given)


def uneven_parts(stream_key, count, total, limit, slope):
    if count == 2:
        one = jax.random.randint(stream_key, (), max(1, total - limit), min(limit, total - 1) + 1)
        return jnp.stack([one, total - one])
    sizes = jnp.asarray(split_up(count, total, limit, slope), jnp.int32)
    pairs = (count - 1) // 2
    donor, taker = sizes[1:1 + 2 * pairs:2], sizes[2:2 + 2 * pairs:2]
    slack = jnp.minimum(donor - 1, limit - taker)
    moved = jax.random.randint(jax.random.fold_in(stream_key, 1), (pairs,), 0, 1 << 20) % (slack + 1)
    sizes = sizes.at[1:1 + 2 * pairs:2].set(donor - moved).at[2:2 + 2 * pairs:2].set(taker + moved)
    return sizes[jax.random.permutation(jax.random.fold_in(stream_key, 2), count)]


def centred(rng, extent, width, bound, shards=(), kind=jnp.bfloat16):
    values = jax.random.normal(rng, extent, jnp.float32) * width
    if len(shards) > 0:
        values = level_of(rng, extent, shards, -0.22, 0.18) * values
    return jnp.clip(values, min=-bound, max=bound).astype(kind)


def bell_draw_with(own_key, shape, spread, reach, pieces, heavy, kind=jnp.bfloat16):
    drawn = spread * jax.random.normal(own_key, shape, jnp.float32)
    if pieces:
        drawn = drawn * level_of(own_key, shape, pieces, -0.22, 0.18)
    return jnp.clip(with_spikes(drawn, jax.random.fold_in(own_key, 3), *heavy), -reach, reach).astype(kind)


def setup_inputs(seed: int = 0, part: int = 0) -> dict:
    streams_of = jax.random.split(jax.random.key(seed), 13)
    own_keys = jax.random.split(jax.random.fold_in(streams_of[12], part), 13)
    feats = centred(own_keys[0], (ROWS, 3 * D), 1.0, 6.0, ((1, 16),))
    uniting_weight = bell_draw_with(streams_of[1], (3 * D, D), (3 * D) ** -0.5, 0.0546875, ((0, 16),), (0, 1, 16, 2.0))
    embeds_verified = centred(own_keys[2], (ROWS, D), 1.0, 6.0, ((1, 16),))
    draft_embeds = centred(own_keys[3], (STEPS, NODES, D), 1.0, 6.0, ((2, 16),))
    gain_embed = jnp.clip(1.0 + 0.15 * jax.random.normal(streams_of[4], (D,), jnp.float32), 0.25, 1.75).astype(jnp.bfloat16)
    gain_hidden = jnp.clip(1.0 + 0.15 * jax.random.normal(streams_of[5], (D,), jnp.float32), 0.25, 1.75).astype(jnp.bfloat16)
    proj_embed = centred(streams_of[6], (D, (QH + 2 * KVH) * HD), D ** -0.5, 0.0625, ((0, 16),))
    proj_hidden = centred(streams_of[7], (D, (QH + 2 * KVH) * HD), D ** -0.5, 0.0625, ((0, 16),))
    out_proj = centred(streams_of[8], (QH * HD, D), (QH * HD) ** -0.5, 0.09375, ((1, 16),))
    lengths = uneven_parts(own_keys[9], SEQS, ROWS, ROWS // 4, 2).astype(jnp.int32)
    root_seq = plant(jax.random.randint(own_keys[10], (NODES,), 0, SEQS), jax.random.fold_in(own_keys[10], 1), 0, SEQS - 1).astype(jnp.int32)
    parents = plant(jax.random.randint(own_keys[11], (STEPS - 1, NODES), 0, NODES), jax.random.fold_in(own_keys[11], 1), 0, NODES - 1).astype(jnp.int32)
    return {"feats": feats, "uniting_weight": uniting_weight, "embeds_verified": embeds_verified, "draft_embeds": draft_embeds, "gain_embed": gain_embed, "gain_hidden": gain_hidden, "proj_embed": proj_embed, "proj_hidden": proj_hidden, "out_proj": out_proj, "lengths": lengths, "root_seq": root_seq, "parents": parents}


def rope_heads(values, positions):
    half = values.shape[-1] // 2
    freq = 500000.0 ** (-(jnp.arange(half, dtype=jnp.float32) * 2.0 / values.shape[-1]))
    angle = positions.astype(jnp.float32)[:, None] * freq[None, :]
    cosine = jnp.cos(angle)[:, None, :]
    sine = jnp.sin(angle)[:, None, :]
    first = values[..., :half]
    second = values[..., half:]
    return jnp.concatenate([first * cosine - second * sine, second * cosine + first * sine], axis=-1)

def scaled_input(values, gain):
    return (values.astype(jnp.float32) * gain.astype(jnp.float32)[None, :]).astype(jnp.bfloat16)

def project_rows(embed_rows, hidden_rows, gain_embed, gain_hidden, w_embed, w_hidden):
    inv_e = lax.rsqrt(lax.optimization_barrier(jnp.sum(embed_rows.astype(jnp.float32) ** 2, axis=-1)) / D + 1e-05)
    inv_h = lax.rsqrt(lax.optimization_barrier(jnp.sum(hidden_rows.astype(jnp.float32) ** 2, axis=-1)) / D + 1e-05)
    part_e = jnp.dot(scaled_input(embed_rows, gain_embed), w_embed, preferred_element_type=jnp.float32)
    part_h = jnp.dot(scaled_input(hidden_rows, gain_hidden), w_hidden, preferred_element_type=jnp.float32)
    return part_e * inv_e[:, None] + part_h * inv_h[:, None]

def attend(queries, keys, values, allowed):
    nodes = queries.shape[0]
    kv_heads = keys.shape[1]
    group = queries.shape[1] // kv_heads
    grouped = queries.reshape(nodes, kv_heads, group, queries.shape[2])
    scores = jnp.einsum('bkgd,nkd->bkgn', grouped.astype(jnp.float32), keys.astype(jnp.float32)) / math.sqrt(queries.shape[2])
    scores = jnp.where(allowed[:, None, None, :], scores, -1e+30)
    top = lax.optimization_barrier(jnp.max(scores, axis=-1, keepdims=True))
    expo = jnp.exp(scores - top)
    weights = (expo / lax.optimization_barrier(jnp.sum(expo, axis=-1, keepdims=True))).astype(jnp.bfloat16)
    mixed = jnp.einsum('bkgn,nkd->bkgd', weights.astype(jnp.float32), values.astype(jnp.float32))
    return mixed.astype(jnp.bfloat16).reshape(nodes, -1)

def reference(feats, uniting_weight, embeds_verified, draft_embeds, gain_embed, gain_hidden, proj_embed, proj_hidden, out_proj, lengths, root_seq, parents):
    ends = jnp.cumsum(lengths).astype(jnp.int32)
    starts = (ends - lengths).astype(jnp.int32)
    row_ids = jnp.arange(ROWS, dtype=jnp.int32)
    seg = lax.optimization_barrier(jnp.sum((row_ids[:, None] >= ends[None, :]).astype(jnp.int32), axis=1)).astype(jnp.int32)
    pos_v = (row_ids - starts[seg]).astype(jnp.int32)
    last = (ends - 1).astype(jnp.int32)
    united = jnp.dot(feats, uniting_weight, preferred_element_type=jnp.float32).astype(jnp.bfloat16)
    qcols = QH * HD
    kcols = KVH * HD
    context = project_rows(embeds_verified, united, gain_embed, gain_hidden, proj_embed[:, qcols:], proj_hidden[:, qcols:])
    keys_v = rope_heads(context[:, :kcols].reshape(ROWS, KVH, HD), pos_v).astype(jnp.bfloat16)
    vals_v = context[:, kcols:].reshape(ROWS, KVH, HD).astype(jnp.bfloat16)
    node_ids = jnp.arange(NODES, dtype=jnp.int32)
    node_keys = []
    node_vals = []
    ancestors = []
    drafts = []
    seq = root_seq
    h_out = united
    for step in range(STEPS):
        if step == 0:
            h_in = jnp.take(united, last[root_seq], axis=0)
        else:
            link = parents[step - 1]
            h_in = jnp.take(h_out, link, axis=0)
            seq = seq[link]
            ancestors = [older[link] for older in ancestors] + [link]
        positions = (lengths[seq] + step).astype(jnp.int32)
        proj = project_rows(draft_embeds[step], h_in, gain_embed, gain_hidden, proj_embed, proj_hidden)
        queries = rope_heads(proj[:, :qcols].reshape(NODES, QH, HD), positions).astype(jnp.bfloat16)
        node_keys.append(rope_heads(proj[:, qcols:qcols + kcols].reshape(NODES, KVH, HD), positions).astype(jnp.bfloat16))
        node_vals.append(proj[:, qcols + kcols:].reshape(NODES, KVH, HD).astype(jnp.bfloat16))
        masks = [seg[None, :] == seq[:, None]]
        for older in ancestors:
            masks.append(older[:, None] == node_ids[None, :])
        masks.append(node_ids[:, None] == node_ids[None, :])
        allowed = jnp.concatenate(masks, axis=1)
        keys = jnp.concatenate([keys_v] + node_keys, axis=0)
        values = jnp.concatenate([vals_v] + node_vals, axis=0)
        mixed = attend(queries, keys, values, allowed)
        h_out = (h_in.astype(jnp.float32) + jnp.dot(mixed, out_proj, preferred_element_type=jnp.float32)).astype(jnp.bfloat16)
        drafts.append(h_out)
    return jnp.concatenate(drafts, axis=0)
```

```python
import functools
import math

import jax
import jax.numpy as jnp
from jax import lax
from jax.experimental import pallas as pl
from jax.experimental.pallas import tpu as pltpu
from jax.sharding import PartitionSpec as P

D = 8192
HD = 128


def rope_heads(values, positions):
    half = values.shape[-1] // 2
    freq = 500000.0 ** (-(jnp.arange(half, dtype=jnp.float32) * 2.0 / values.shape[-1]))
    angle = positions.astype(jnp.float32)[:, None] * freq[None, :]
    cosine = jnp.cos(angle)[:, None, :]
    sine = jnp.sin(angle)[:, None, :]
    first = values[..., :half]
    second = values[..., half:]
    return jnp.concatenate(
        [first * cosine - second * sine, second * cosine + first * sine], axis=-1
    )


def scaled_input(values, gain):
    return (values.astype(jnp.float32) * gain.astype(jnp.float32)[None, :]).astype(jnp.bfloat16)


def project_rows(embed_rows, hidden_rows, gain_embed, gain_hidden, w_embed, w_hidden):
    part_e = jnp.dot(
        scaled_input(embed_rows, gain_embed), w_embed, preferred_element_type=jnp.float32
    )
    part_h = jnp.dot(
        scaled_input(hidden_rows, gain_hidden), w_hidden, preferred_element_type=jnp.float32
    )
    square_e = jnp.sum(embed_rows.astype(jnp.float32) ** 2, axis=-1)
    square_h = jnp.sum(hidden_rows.astype(jnp.float32) ** 2, axis=-1)
    total_e, total_h = lax.psum((square_e, square_h), "section")
    inv_e = lax.rsqrt(total_e / D + 1e-05)
    inv_h = lax.rsqrt(total_h / D + 1e-05)
    return lax.psum(part_e * inv_e[:, None] + part_h * inv_h[:, None], "section")


def attend(queries, keys, values, allowed):
    nodes = queries.shape[0]
    kv_heads = keys.shape[1]
    group = queries.shape[1] // kv_heads
    grouped = queries.reshape(nodes, kv_heads, group, queries.shape[2])
    scores = jnp.einsum(
        "bkgd,nkd->bkgn", grouped, keys, preferred_element_type=jnp.float32
    ) / math.sqrt(queries.shape[2])
    scores = jnp.where(allowed[:, None, None, :], scores, -1e30)
    top = jnp.max(scores, axis=-1, keepdims=True)
    expo = jnp.exp(scores - top)
    weights = (expo / jnp.sum(expo, axis=-1, keepdims=True)).astype(jnp.bfloat16)
    mixed = jnp.einsum("bkgn,nkd->bkgd", weights, values, preferred_element_type=jnp.float32)
    return mixed.astype(jnp.bfloat16).reshape(nodes, -1)


def local_plain(
    feats,
    uniting_weight,
    embeds_verified,
    draft_embeds,
    gain_embed,
    gain_hidden,
    proj_embed,
    proj_hidden,
    out_proj,
    lengths,
    root_seq,
    parents,
):
    row_count = feats.shape[0]
    node_count = draft_embeds.shape[1]
    step_count = draft_embeds.shape[0]
    qcols = out_proj.shape[0]
    kcols = (proj_embed.shape[1] - qcols) // 2
    q_heads = qcols // HD
    kv_heads = kcols // HD
    ends = jnp.cumsum(lengths)
    starts = ends - lengths
    row_ids = jnp.arange(row_count, dtype=jnp.int32)
    seg = jnp.sum((row_ids[:, None] >= ends[None, :]).astype(jnp.int32), axis=1)
    pos_v = row_ids - starts[seg]
    last = ends - 1
    partial_value = jnp.dot(feats, uniting_weight, preferred_element_type=jnp.float32)
    united = lax.psum_scatter(partial_value, "section", scatter_dimension=1, tiled=True).astype(
        jnp.bfloat16
    )
    context = project_rows(
        embeds_verified,
        united,
        gain_embed,
        gain_hidden,
        proj_embed[:, qcols:],
        proj_hidden[:, qcols:],
    )
    keys_v = rope_heads(context[:, :kcols].reshape(row_count, kv_heads, HD), pos_v).astype(
        jnp.bfloat16
    )
    vals_v = context[:, kcols:].reshape(row_count, kv_heads, HD).astype(jnp.bfloat16)
    node_ids = jnp.arange(node_count, dtype=jnp.int32)
    node_keys = []
    node_vals = []
    ancestors = []
    drafts = []
    seq = root_seq
    h_out = united
    for step in range(step_count):
        if step == 0:
            h_in = jnp.take(united, last[root_seq], axis=0)
        else:
            link = parents[step - 1]
            h_in = jnp.take(h_out, link, axis=0)
            seq = seq[link]
            ancestors = [older[link] for older in ancestors] + [link]
        positions = lengths[seq] + step
        proj = project_rows(
            draft_embeds[step], h_in, gain_embed, gain_hidden, proj_embed, proj_hidden
        )
        queries = rope_heads(proj[:, :qcols].reshape(node_count, q_heads, HD), positions).astype(
            jnp.bfloat16
        )
        node_keys.append(
            rope_heads(
                proj[:, qcols : qcols + kcols].reshape(node_count, kv_heads, HD), positions
            ).astype(jnp.bfloat16)
        )
        node_vals.append(
            proj[:, qcols + kcols :].reshape(node_count, kv_heads, HD).astype(jnp.bfloat16)
        )
        masks = [seg[None, :] == seq[:, None]]
        for older in ancestors:
            masks.append(older[:, None] == node_ids[None, :])
        masks.append(node_ids[:, None] == node_ids[None, :])
        allowed = jnp.concatenate(masks, axis=1)
        keys = jnp.concatenate([keys_v] + node_keys, axis=0)
        values = jnp.concatenate([vals_v] + node_vals, axis=0)
        mixed = attend(queries, keys, values, allowed)
        h_out = (
            h_in.astype(jnp.float32) + jnp.dot(mixed, out_proj, preferred_element_type=jnp.float32)
        ).astype(jnp.bfloat16)
        drafts.append(h_out)
    columns = jnp.concatenate(drafts, axis=0)
    return lax.all_to_all(columns, "section", split_axis=0, concat_axis=1, tiled=True)


Z, Y, C = 4, 2, 2
N = Z * Y * C
MASKED = -1e30


def remote(src, dst, send, recv, peer):
    return pltpu.make_async_remote_copy(
        src_ref=src,
        dst_ref=dst,
        send_sem=send,
        recv_sem=recv,
        device_id={"section": peer},
        device_id_type=pl.DeviceIdType.MESH,
    )


def column_to_row(column):
    rows = lax.broadcasted_iota(jnp.int32, (column.shape[0], column.shape[0]), 0)
    cols = lax.broadcasted_iota(jnp.int32, (column.shape[0], column.shape[0]), 1)
    return jnp.sum(jnp.where(rows == cols, column, 0.0), axis=0, keepdims=True)


def row_to_column(pick, row):
    return jnp.sum(jnp.where(pick > 0, row, 0.0), axis=1, keepdims=True)


def draft_kernel(
    steps,
    partial_ref,
    eg_ref,
    sqe_ref,
    gh_ref,
    we_ref,
    wh_ref,
    wo_ref,
    pick_ref,
    mask_ref,
    cos_ref,
    sin_ref,
    out_ref,
    h_ref,
    hg_ref,
    part_ref,
    kvp_ref,
    own_ref,
    cs_ref,
    cr_ref,
    ys_ref,
    yr_ref,
    zs_ref,
    zr_ref,
    uown_ref,
    ucs_ref,
    ucr_ref,
    uys_ref,
    uyr_ref,
    uzs_ref,
    uzr_ref,
    sqs_ref,
    sqr_ref,
    kv_ref,
    att_ref,
    sum_ref,
    inve_ref,
    cs_sem,
    cr_sem,
    ys_sem,
    yr_sem,
    zs_sem,
    zr_sem,
    sqs_sem,
    sqr_sem,
    kvs_sem,
    kvr_sem,
    ags_sem,
    agr_sem,
):
    rows, width = h_ref.shape
    me = lax.axis_index("section")
    z = me // 4
    y = (me // 2) % 2
    c = me % 2
    yc = me % 4
    sibling = z * 4 + y * 2 + (1 - c)
    y_peer = z * 4 + (1 - y) * 2 + c
    quarter = rows // 4
    qcols = wo_ref.shape[0]
    kcols = (we_ref.shape[1] - qcols) // 2
    block_cols = qcols // N
    f32, bf16 = jnp.float32, jnp.bfloat16

    kv_ref[...] = jnp.zeros_like(kv_ref)

    barrier = pltpu.get_barrier_semaphore()

    def greet(k, _):
        pl.semaphore_signal(
            barrier,
            inc=1,
            device_id={"section": (me + k) % N},
            device_id_type=pl.DeviceIdType.MESH,
        )
        return 0

    lax.fori_loop(1, N, greet, 0)
    pl.semaphore_wait(barrier, N - 1)

    def squares_copy(slot, k, peer, source):
        return remote(
            sqs_ref.at[slot],
            sqr_ref.at[slot, source],
            sqs_sem.at[slot, k],
            sqr_sem.at[slot, source],
            peer,
        )

    def squares_start(slot, value):
        sqs_ref[slot] = value
        sqr_ref[slot, me] = value

        def go(k, _):
            squares_copy(slot, k, (me + k) % N, me).start()
            return 0

        lax.fori_loop(1, N, go, 0)

    def squares_total(slot):
        def go(k, total):
            source = (me + k) % N
            copy = squares_copy(slot, k, source, source)
            copy.wait_recv()
            copy.wait_send()
            return total + sqr_ref[slot, source]

        return lax.fori_loop(1, N, go, sqr_ref[slot, me])

    def reduce_scatter(s, t, size, block, own, cs, cr, ys, yr, zs, zr):
        def order(k):
            far = k < 4
            return jnp.where(far, k, k - 4), jnp.where(far, 1 - y, y)

        def core_copy(k):
            return remote(
                cs.at[k, pl.ds(0, size)], cr.at[t, k, pl.ds(0, size)], cs_sem.at[s, k],
                cr_sem.at[s, k], sibling,
            )

        def y_copy(k):
            return remote(
                ys.at[k, pl.ds(0, size)], yr.at[t, k, pl.ds(0, size)], ys_sem.at[s, k],
                yr_sem.at[s, k], y_peer,
            )

        def z_copy(k):
            other = (z + k) % Z
            return remote(
                zs.at[k, pl.ds(0, size)], zr.at[t, k, pl.ds(0, size)], zs_sem.at[s, k],
                zr_sem.at[s, k], other * 4 + yc,
            )

        def give(k, _):
            zb, yb = order(k)
            block(zb, yb, 1 - c, cs.at[k], bf16)
            core_copy(k).start()
            return 0

        lax.fori_loop(0, 8, give, 0)

        def keep(k, _):
            zb, yb = order(k)
            block(zb, yb, c, own.at[k], f32)
            return 0

        lax.fori_loop(0, 8, keep, 0)

        def across(k, _):
            core_copy(k).wait_recv()
            ys[k, 0:size] = (own[k, 0:size] + cr[t, k, 0:size].astype(f32)).astype(bf16)
            y_copy(k).start()
            return 0

        lax.fori_loop(0, 4, across, 0)

        def near(k, _):
            core_copy(k).wait_recv()
            own[k, 0:size] = own[k, 0:size] + cr[t, k, 0:size].astype(f32)
            return 0

        lax.fori_loop(4, 8, near, 0)

        def along(j, _):
            k = j % Z
            zb = (z + k) % Z
            y_copy(zb).wait_recv()
            value = own[4 + zb, 0:size] + yr[t, zb, 0:size].astype(f32)

            @pl.when(k != 0)
            def _():
                zs[k, 0:size] = value.astype(bf16)
                z_copy(k).start()

            @pl.when(k == 0)
            def _():
                own[0, 0:size] = value

            return 0

        lax.fori_loop(1, Z + 1, along, 0)

        def collect(k, total):
            z_copy(k).wait_recv()
            return total + zr[t, k, 0:size].astype(f32)

        total = lax.fori_loop(1, Z, collect, own[0, 0:size])

        def drain(k, _):
            core_copy(k).wait_send()
            return 0

        lax.fori_loop(0, 8, drain, 0)

        def drain_y(k, _):
            y_copy(k).wait_send()
            return 0

        lax.fori_loop(0, 4, drain_y, 0)

        def drain_z(k, _):
            z_copy(k).wait_send()
            return 0

        lax.fori_loop(1, Z, drain_z, 0)
        return total

    def squares_of(values):
        wide = values.astype(f32)
        column = jnp.sum(wide * wide, axis=1, keepdims=True)
        return jnp.broadcast_to(column_to_row(column), (8, rows))

    def inverse(total):
        return lax.rsqrt(total / D + 1e-05)

    squares_start(steps, sqe_ref[...])

    def united_block(zb, yb, cb, dst, kind):
        at = pl.multiple_of((zb * 4 + yb * 2 + cb) * width, 128)
        dst[...] = partial_ref[:, pl.ds(at, width)].astype(kind)

    united = reduce_scatter(
        steps, 0, rows, united_block, uown_ref, ucs_ref, ucr_ref, uys_ref, uyr_ref, uzs_ref, uzr_ref
    ).astype(bf16)
    h_ref[...] = united
    inve_ref[...] = inverse(squares_total(steps))
    squares_start(0, squares_of(united))

    eye = (
        lax.broadcasted_iota(jnp.int32, (rows, rows), 0)
        == lax.broadcasted_iota(jnp.int32, (rows, rows), 1)
    ).astype(f32)

    def rope(values, cosine, sine):
        return values * cosine + pltpu.roll(values, HD // 2, 1) * sine

    def project(e, hg, at, size):
        pe = jnp.dot(e, we_ref[:, pl.ds(at, size)], preferred_element_type=f32)
        ph = jnp.dot(hg, wh_ref[:, pl.ds(at, size)], preferred_element_type=f32)
        return pe, ph

    def kv_copy(slot, base, source, k):
        return remote(
            kv_ref.at[pl.ds(base + source * quarter, quarter)],
            kv_ref.at[pl.ds(base + source * quarter, quarter)],
            kvs_sem.at[slot, k],
            kvr_sem.at[slot, source],
            z * 4 + (yc + k) % 4,
        )

    def kv_put(slot, base, values, table):
        off = pl.multiple_of(yc * quarter, 8)
        cosine = cos_ref[table, pl.ds(off, quarter), :]
        sine = sin_ref[table, pl.ds(off, quarter), :]
        where = pl.ds(pl.multiple_of(base + yc * quarter, quarter), quarter)
        kv_ref[where, 0:HD] = rope(values[:, 0:HD], cosine, sine).astype(bf16)
        kv_ref[where, HD : 2 * HD] = values[:, HD : 2 * HD].astype(bf16)
        for k in range(1, 4):
            kv_copy(slot, base, yc, k).start()

    def kv_get(slot, base):
        for k in range(1, 4):
            kv_copy(slot, base, (yc + k) % 4, k).wait_recv()
            kv_copy(slot, base, yc, k).wait_send()

    def gather_copy(t, k, source, peer):
        return remote(
            att_ref.at[t, source], att_ref.at[t, source], ags_sem.at[t, k],
            agr_sem.at[t, source], peer,
        )

    def step(t, first):
        pick = pick_ref[t]
        h_in = jnp.dot(pick, h_ref[...], preferred_element_type=f32).astype(bf16)
        gain = gh_ref[0:1, :].astype(f32)
        hg = (h_in.astype(f32) * gain).astype(bf16)
        hg_ref[...] = hg
        eg = eg_ref[t]
        inv = inverse(squares_total(t))[0:1]
        inv_h = row_to_column(pick, inv)
        row_pick = (lax.broadcasted_iota(jnp.int32, (8, rows), 0) == t).astype(f32)
        inv_e = row_to_column(eye, jnp.sum(inve_ref[...] * row_pick, axis=0, keepdims=True))
        for half in range(2):
            pe, ph = project(eg, hg, qcols + half * kcols, kcols)
            kvp_ref[0, :, half * kcols : (half + 1) * kcols] = pe * inv_e + ph * inv_h
        if first:
            inv_u = row_to_column(eye, inv)
            inv_v = row_to_column(eye, inve_ref[steps : steps + 1, :])
            ug = (h_ref[...].astype(f32) * gain).astype(bf16)
            for half in range(2):
                pe, ph = project(eg_ref[steps], ug, qcols + half * kcols, kcols)
                kvp_ref[1, :, half * kcols : (half + 1) * kcols] = pe * inv_v + ph * inv_u

        def block(zb, yb, cb, dst, kind):
            b = zb * 4 + yb * 2 + cb
            pe, ph = project(
                eg_ref[t], hg_ref[...], pl.multiple_of(b * block_cols, 128), block_cols
            )
            dst[0:rows, :] = (pe * inv_e + ph * inv_h).astype(kind)
            off = pl.multiple_of((yb * 2 + cb) * quarter, 8)
            for which in range(2 if first else 1):
                for half in range(2):
                    at = pl.multiple_of(half * kcols + zb * HD, 128)
                    dst[
                        rows + which * quarter : rows + (which + 1) * quarter,
                        half * HD : (half + 1) * HD,
                    ] = kvp_ref[which, pl.ds(off, quarter), pl.ds(at, HD)].astype(kind)

        size = rows + (2 if first else 1) * quarter
        total = reduce_scatter(
            t, t, size, block, own_ref, cs_ref, cr_ref, ys_ref, yr_ref, zs_ref, zr_ref
        )
        sum_ref[0:size] = total
        base = rows + t * rows
        kv_put(t, base, sum_ref[rows : rows + quarter], t)
        if first:
            kv_put(steps, 0, sum_ref[rows + quarter : rows + 2 * quarter], steps)
        cosine, sine = cos_ref[t], sin_ref[t]
        queries = [
            rope(sum_ref[0:rows, j * HD : (j + 1) * HD], cosine, sine).astype(bf16)
            for j in range(block_cols // HD)
        ]
        kv_get(t, base)
        if first:
            kv_get(steps, 0)
        allowed = mask_ref[t] > 0
        keys = kv_ref[:, 0:HD]
        vals = kv_ref[:, HD : 2 * HD]
        for j, query in enumerate(queries):
            scores = lax.dot_general(
                query, keys, (((1,), (1,)), ((), ())), preferred_element_type=f32
            ) / math.sqrt(HD)
            scores = jnp.where(allowed, scores, MASKED)
            expo = jnp.exp(scores - jnp.max(scores, axis=1, keepdims=True))
            weights = (expo / jnp.sum(expo, axis=1, keepdims=True)).astype(bf16)
            att_ref[t, me, :, j * HD : (j + 1) * HD] = jnp.dot(
                weights, vals, preferred_element_type=f32
            ).astype(bf16)

        for k in range(1, Z):
            gather_copy(t, k, me, ((z + k) % Z) * 4 + yc).start()
        gather_copy(t, 4, me, y_peer).start()
        gather_copy(t, 8, me, sibling).start()

        def product(source):
            at = pl.multiple_of(source * block_cols, 128)
            return jnp.dot(
                att_ref[t, source], wo_ref[pl.ds(at, block_cols), :], preferred_element_type=f32
            )

        part_ref[...] = h_in.astype(f32) + product(me)
        for k in range(1, Z):
            source = ((z + k) % Z) * 4 + yc
            gather_copy(t, k, source, source).wait_recv()
            gather_copy(t, 4 + k, source, y_peer).start()
            gather_copy(t, 8 + k, source, sibling).start()
            part_ref[...] += product(source)
        for k in range(Z):
            source = ((z + k) % Z) * 4 + (1 - y) * 2 + c
            gather_copy(t, 4 + k, source, y_peer).wait_recv()
            gather_copy(t, 12 + k, source, sibling).start()
            part_ref[...] += product(source)
        for yk in range(2):
            for k in range(Z):
                source = ((z + k) % Z) * 4 + ((y + yk) % 2) * 2 + (1 - c)
                gather_copy(t, 8 + 4 * yk + k, source, sibling).wait_recv()
                part_ref[...] += product(source)
        for k in range(1, 16):
            gather_copy(t, k, me, sibling).wait_send()
        h_out = part_ref[...].astype(bf16)
        h_ref[...] = h_out
        out_ref[pl.ds(pl.multiple_of(t * rows, 128), rows), :] = h_out
        return h_out

    h_out = step(0, True)

    def later(t, _):
        squares_start(t, squares_of(h_ref[...]))
        step(t, False)
        return 0

    lax.fori_loop(1, steps, later, 0)


def local_kernel(
    feats,
    uniting_weight,
    embeds_verified,
    draft_embeds,
    gain_embed,
    gain_hidden,
    proj_embed,
    proj_hidden,
    out_proj,
    lengths,
    root_seq,
    parents,
):
    rows = feats.shape[0]
    steps = draft_embeds.shape[0]
    width = out_proj.shape[1]
    qcols = out_proj.shape[0]
    kcols = (proj_embed.shape[1] - qcols) // 2
    block_cols = qcols // N
    f32, bf16 = jnp.float32, jnp.bfloat16
    ends = jnp.cumsum(lengths)
    starts = ends - lengths
    ids = jnp.arange(rows, dtype=jnp.int32)
    slots = jnp.arange(lengths.shape[0], dtype=jnp.int32)
    seg = jnp.sum((ids[:, None] >= ends[None, :]).astype(jnp.int32), axis=1)
    of_seg = seg[:, None] == slots[None, :]
    pos_v = ids - jnp.sum(jnp.where(of_seg, starts[None, :], 0), axis=1)

    def look(table, index, count):
        hit = index[:, None] == jnp.arange(count, dtype=jnp.int32)[None, :]
        return jnp.sum(jnp.where(hit, table[None, :], 0), axis=1)

    seq = root_seq
    picks, masks, positions = [], [], []
    ancestors = []
    none = jnp.zeros((rows, rows), jnp.bool_)
    for t in range(steps):
        if t == 0:
            link = look(ends - 1, root_seq, lengths.shape[0])
        else:
            link = parents[t - 1]
            seq = look(seq, link, rows)
            ancestors = [look(older, link, rows) for older in ancestors] + [link]
        picks.append(link[:, None] == ids[None, :])
        positions.append(look(lengths, seq, lengths.shape[0]) + t)
        mask = [seg[None, :] == seq[:, None]]
        mask += [older[:, None] == ids[None, :] for older in ancestors]
        mask.append(ids[:, None] == ids[None, :])
        mask += [none] * (steps + 1 - len(mask))
        masks.append(jnp.concatenate(mask, axis=1))
    positions.append(pos_v)
    pick = jnp.stack(picks).astype(bf16)
    mask = jnp.stack(masks).astype(f32)
    half = HD // 2
    freq = 500000.0 ** (-(jnp.arange(half, dtype=f32) * 2.0 / HD))
    angle = jnp.stack(positions).astype(f32)[:, :, None] * freq[None, None, :]
    cosine, sine = jnp.cos(angle), jnp.sin(angle)
    cosine = jnp.concatenate([cosine, cosine], axis=-1)
    sine = jnp.concatenate([-sine, sine], axis=-1)
    embeds = jnp.concatenate([draft_embeds, embeds_verified[None]], axis=0)
    wide = embeds.astype(f32)
    eg = (wide * gain_embed.astype(f32)[None, None, :]).astype(bf16)
    sqe = jnp.sum(wide * wide, axis=-1)
    sqe = jnp.concatenate([sqe, jnp.zeros((8 - steps - 1, rows), f32)], axis=0)
    gh = jnp.broadcast_to(gain_hidden[None, :], (16, width))
    partial_value = jnp.dot(feats, uniting_weight, preferred_element_type=f32)
    tall = rows + rows // 2
    vmem = pl.BlockSpec(memory_space=pltpu.VMEM)
    dma = pltpu.SemaphoreType.DMA
    columns = pl.pallas_call(
        functools.partial(draft_kernel, steps),
        out_shape=jax.ShapeDtypeStruct((steps * rows, width), bf16),
        in_specs=[vmem] * 11,
        out_specs=vmem,
        scratch_shapes=[
            pltpu.VMEM((rows, width), bf16),
            pltpu.VMEM((rows, width), bf16),
            pltpu.VMEM((rows, width), f32),
            pltpu.VMEM((2, rows, 2 * kcols), f32),
            pltpu.VMEM((8, tall, block_cols), f32),
            pltpu.VMEM((8, tall, block_cols), bf16),
            pltpu.VMEM((steps, 8, tall, block_cols), bf16),
            pltpu.VMEM((4, tall, block_cols), bf16),
            pltpu.VMEM((steps, 4, tall, block_cols), bf16),
            pltpu.VMEM((4, tall, block_cols), bf16),
            pltpu.VMEM((steps, 4, tall, block_cols), bf16),
            pltpu.VMEM((8, rows, width), f32),
            pltpu.VMEM((8, rows, width), bf16),
            pltpu.VMEM((1, 8, rows, width), bf16),
            pltpu.VMEM((4, rows, width), bf16),
            pltpu.VMEM((1, 4, rows, width), bf16),
            pltpu.VMEM((4, rows, width), bf16),
            pltpu.VMEM((1, 4, rows, width), bf16),
            pltpu.VMEM((steps + 1, 8, rows), f32),
            pltpu.VMEM((steps + 1, N, 8, rows), f32),
            pltpu.VMEM(((steps + 1) * rows, 2 * HD), bf16),
            pltpu.VMEM((steps, N, rows, block_cols), bf16),
            pltpu.VMEM((tall, block_cols), f32),
            pltpu.VMEM((8, rows), f32),
            dma((steps + 1, 8)),
            dma((steps + 1, 8)),
            dma((steps + 1, 4)),
            dma((steps + 1, 4)),
            dma((steps + 1, 4)),
            dma((steps + 1, 4)),
            dma((steps + 1, N)),
            dma((steps + 1, N)),
            dma((steps + 1, 4)),
            dma((steps + 1, 4)),
            dma((steps, N)),
            dma((steps, N)),
        ],
        compiler_params=pltpu.CompilerParams(
            collective_id=0, has_side_effects=True, vmem_limit_bytes=60 * 1024 * 1024
        ),
    )(partial_value, eg, sqe, gh, proj_embed, proj_hidden, out_proj, pick, mask, cosine, sine)
    return lax.all_to_all(columns, "section", split_axis=0, concat_axis=1, tiled=True)


def solution(mesh):
    return jax.shard_map(
        local_kernel if mesh.shape["section"] == N else local_plain,
        mesh=mesh,
        in_specs=(
            P("groups", "section"),
            P("section", None),
            P("groups", "section"),
            P(None, "groups", "section"),
            P("section"),
            P("section"),
            P("section", None),
            P("section", None),
            P(None, "section"),
            P("groups"),
            P("groups"),
            P(None, "groups"),
        ),
        out_specs=P(("groups", "section"), None),
        check_vma=False,
    )
```

```python
import functools
import math

import jax
import jax.numpy as jnp
from jax import lax
from jax.experimental import pallas as pl
from jax.experimental.pallas import tpu as pltpu
from jax.sharding import PartitionSpec as P

D = 8192
HD = 128


def rope_heads(values, positions):
    half = values.shape[-1] // 2
    freq = 500000.0 ** (-(jnp.arange(half, dtype=jnp.float32) * 2.0 / values.shape[-1]))
    angle = positions.astype(jnp.float32)[:, None] * freq[None, :]
    cosine = jnp.cos(angle)[:, None, :]
    sine = jnp.sin(angle)[:, None, :]
    first = values[..., :half]
    second = values[..., half:]
    return jnp.concatenate(
        [first * cosine - second * sine, second * cosine + first * sine], axis=-1
    )


def scaled_input(values, gain):
    return (values.astype(jnp.float32) * gain.astype(jnp.float32)[None, :]).astype(jnp.bfloat16)


def project_rows(embed_rows, hidden_rows, gain_embed, gain_hidden, w_embed, w_hidden):
    part_e = jnp.dot(
        scaled_input(embed_rows, gain_embed), w_embed, preferred_element_type=jnp.float32
    )
    part_h = jnp.dot(
        scaled_input(hidden_rows, gain_hidden), w_hidden, preferred_element_type=jnp.float32
    )
    square_e = jnp.sum(embed_rows.astype(jnp.float32) ** 2, axis=-1)
    square_h = jnp.sum(hidden_rows.astype(jnp.float32) ** 2, axis=-1)
    total_e, total_h = lax.psum((square_e, square_h), "section")
    inv_e = lax.rsqrt(total_e / D + 1e-05)
    inv_h = lax.rsqrt(total_h / D + 1e-05)
    return lax.psum(part_e * inv_e[:, None] + part_h * inv_h[:, None], "section")


def attend(queries, keys, values, allowed):
    nodes = queries.shape[0]
    kv_heads = keys.shape[1]
    group = queries.shape[1] // kv_heads
    grouped = queries.reshape(nodes, kv_heads, group, queries.shape[2])
    scores = jnp.einsum(
        "bkgd,nkd->bkgn", grouped, keys, preferred_element_type=jnp.float32
    ) / math.sqrt(queries.shape[2])
    scores = jnp.where(allowed[:, None, None, :], scores, -1e30)
    top = jnp.max(scores, axis=-1, keepdims=True)
    expo = jnp.exp(scores - top)
    weights = (expo / jnp.sum(expo, axis=-1, keepdims=True)).astype(jnp.bfloat16)
    mixed = jnp.einsum("bkgn,nkd->bkgd", weights, values, preferred_element_type=jnp.float32)
    return mixed.astype(jnp.bfloat16).reshape(nodes, -1)


def local_plain(
    feats,
    uniting_weight,
    embeds_verified,
    draft_embeds,
    gain_embed,
    gain_hidden,
    proj_embed,
    proj_hidden,
    out_proj,
    lengths,
    root_seq,
    parents,
):
    row_count = feats.shape[0]
    node_count = draft_embeds.shape[1]
    step_count = draft_embeds.shape[0]
    qcols = out_proj.shape[0]
    kcols = (proj_embed.shape[1] - qcols) // 2
    q_heads = qcols // HD
    kv_heads = kcols // HD
    ends = jnp.cumsum(lengths)
    starts = ends - lengths
    row_ids = jnp.arange(row_count, dtype=jnp.int32)
    seg = jnp.sum((row_ids[:, None] >= ends[None, :]).astype(jnp.int32), axis=1)
    pos_v = row_ids - starts[seg]
    last = ends - 1
    partial_value = jnp.dot(feats, uniting_weight, preferred_element_type=jnp.float32)
    united = lax.psum_scatter(partial_value, "section", scatter_dimension=1, tiled=True).astype(
        jnp.bfloat16
    )
    context = project_rows(
        embeds_verified,
        united,
        gain_embed,
        gain_hidden,
        proj_embed[:, qcols:],
        proj_hidden[:, qcols:],
    )
    keys_v = rope_heads(context[:, :kcols].reshape(row_count, kv_heads, HD), pos_v).astype(
        jnp.bfloat16
    )
    vals_v = context[:, kcols:].reshape(row_count, kv_heads, HD).astype(jnp.bfloat16)
    node_ids = jnp.arange(node_count, dtype=jnp.int32)
    node_keys = []
    node_vals = []
    ancestors = []
    drafts = []
    seq = root_seq
    h_out = united
    for step in range(step_count):
        if step == 0:
            h_in = jnp.take(united, last[root_seq], axis=0)
        else:
            link = parents[step - 1]
            h_in = jnp.take(h_out, link, axis=0)
            seq = seq[link]
            ancestors = [older[link] for older in ancestors] + [link]
        positions = lengths[seq] + step
        proj = project_rows(
            draft_embeds[step], h_in, gain_embed, gain_hidden, proj_embed, proj_hidden
        )
        queries = rope_heads(proj[:, :qcols].reshape(node_count, q_heads, HD), positions).astype(
            jnp.bfloat16
        )
        node_keys.append(
            rope_heads(
                proj[:, qcols : qcols + kcols].reshape(node_count, kv_heads, HD), positions
            ).astype(jnp.bfloat16)
        )
        node_vals.append(
            proj[:, qcols + kcols :].reshape(node_count, kv_heads, HD).astype(jnp.bfloat16)
        )
        masks = [seg[None, :] == seq[:, None]]
        for older in ancestors:
            masks.append(older[:, None] == node_ids[None, :])
        masks.append(node_ids[:, None] == node_ids[None, :])
        allowed = jnp.concatenate(masks, axis=1)
        keys = jnp.concatenate([keys_v] + node_keys, axis=0)
        values = jnp.concatenate([vals_v] + node_vals, axis=0)
        mixed = attend(queries, keys, values, allowed)
        h_out = (
            h_in.astype(jnp.float32) + jnp.dot(mixed, out_proj, preferred_element_type=jnp.float32)
        ).astype(jnp.bfloat16)
        drafts.append(h_out)
    columns = jnp.concatenate(drafts, axis=0)
    return lax.all_to_all(columns, "section", split_axis=0, concat_axis=1, tiled=True)


Z, Y, C = 4, 2, 2
N = Z * Y * C
MASKED = -1e30


def remote(src, dst, send, recv, peer):
    return pltpu.make_async_remote_copy(
        src_ref=src,
        dst_ref=dst,
        send_sem=send,
        recv_sem=recv,
        device_id={"section": peer},
        device_id_type=pl.DeviceIdType.MESH,
    )


def column_to_row(column):
    rows = lax.broadcasted_iota(jnp.int32, (column.shape[0], column.shape[0]), 0)
    cols = lax.broadcasted_iota(jnp.int32, (column.shape[0], column.shape[0]), 1)
    return jnp.sum(jnp.where(rows == cols, column, 0.0), axis=0, keepdims=True)


def row_to_column(pick, row):
    return jnp.sum(jnp.where(pick > 0, row, 0.0), axis=1, keepdims=True)


def draft_kernel(
    steps,
    feats_ref,
    uniting_ref,
    eg_ref,
    sqe_ref,
    gh_ref,
    we_hbm,
    wh_hbm,
    wo_hbm,
    pick_ref,
    mask_ref,
    cos_ref,
    sin_ref,
    out_ref,
    we_ref,
    wh_ref,
    wo_ref,
    strip_ref,
    pe_ref,
    ctx_ref,
    hist_ref,
    rows_ref,
    strip_sem,
    weight_sem,
    outs_sem,
    outr_sem,
    h_ref,
    hg_ref,
    part_ref,
    kvp_ref,
    own_ref,
    cs_ref,
    cr_ref,
    ys_ref,
    yr_ref,
    zs_ref,
    zr_ref,
    uown_ref,
    ucs_ref,
    ucr_ref,
    uys_ref,
    uyr_ref,
    uzs_ref,
    uzr_ref,
    sqs_ref,
    sqr_ref,
    kv_ref,
    att_ref,
    sum_ref,
    inve_ref,
    cs_sem,
    cr_sem,
    ys_sem,
    yr_sem,
    zs_sem,
    zr_sem,
    sqs_sem,
    sqr_sem,
    kvs_sem,
    kvr_sem,
    ags_sem,
    agr_sem,
):
    rows, width = h_ref.shape
    me = lax.axis_index("section")
    z = me // 4
    y = (me // 2) % 2
    c = me % 2
    yc = me % 4
    sibling = z * 4 + y * 2 + (1 - c)
    y_peer = z * 4 + (1 - y) * 2 + c
    quarter = rows // 4
    qcols = wo_ref.shape[0]
    kcols = (we_ref.shape[1] - qcols) // 2
    block_cols = qcols // N
    f32, bf16 = jnp.float32, jnp.bfloat16

    kv_ref[...] = jnp.zeros_like(kv_ref)

    barrier = pltpu.get_barrier_semaphore()

    def greet(k, _):
        pl.semaphore_signal(
            barrier,
            inc=1,
            device_id={"section": (me + k) % N},
            device_id_type=pl.DeviceIdType.MESH,
        )
        return 0

    lax.fori_loop(1, N, greet, 0)
    pl.semaphore_wait(barrier, N - 1)

    def squares_copy(slot, k, peer, source):
        return remote(
            sqs_ref.at[slot],
            sqr_ref.at[slot, source],
            sqs_sem.at[slot, k],
            sqr_sem.at[slot, source],
            peer,
        )

    def squares_start(slot, value):
        sqs_ref[slot] = value
        sqr_ref[slot, me] = value

        def go(k, _):
            squares_copy(slot, k, (me + k) % N, me).start()
            return 0

        lax.fori_loop(1, N, go, 0)

    def squares_total(slot):
        def go(k, total):
            source = (me + k) % N
            copy = squares_copy(slot, k, source, source)
            copy.wait_recv()
            copy.wait_send()
            return total + sqr_ref[slot, source]

        return lax.fori_loop(1, N, go, sqr_ref[slot, me])

    def reduce_scatter(s, t, size, block, own, cs, cr, ys, yr, zs, zr, meanwhile=None):
        def order(k):
            far = k < 4
            return (z + 1 + jnp.where(far, k, k - 4)) % Z, jnp.where(far, 1 - y, y)

        def core_copy(k):
            return remote(
                cs.at[k, pl.ds(0, size)], cr.at[t, k, pl.ds(0, size)], cs_sem.at[s, k],
                cr_sem.at[s, k], sibling,
            )

        def y_copy(k):
            return remote(
                ys.at[k, pl.ds(0, size)], yr.at[t, k, pl.ds(0, size)], ys_sem.at[s, k],
                yr_sem.at[s, k], y_peer,
            )

        def z_copy(k):
            return remote(
                zs.at[k, pl.ds(0, size)], zr.at[t, k, pl.ds(0, size)], zs_sem.at[s, k],
                zr_sem.at[s, k], ((z + 1 + k) % Z) * 4 + yc,
            )

        def give(k, _):
            zb, yb = order(k)
            block(zb, yb, 1 - c, cs.at[k], bf16, k + jnp.where(k < 4, 0, 4))
            core_copy(k).start()
            return 0

        def keep(k, _):
            zb, yb = order(k)
            block(zb, yb, c, own.at[k], f32, k + jnp.where(k < 4, 4, 8))
            return 0

        def across(k, _):
            keep(k, 0)
            core_copy(k).wait_recv()
            ys[k, 0:size] = (own[k, 0:size] + cr[t, k, 0:size].astype(f32)).astype(bf16)
            y_copy(k).start()
            return 0

        lax.fori_loop(0, 4, give, 0)
        lax.fori_loop(0, 4, across, 0)
        lax.fori_loop(4, 8, give, 0)
        lax.fori_loop(4, 8, keep, 0)

        def along(k, _):
            core_copy(k + 4).wait_recv()
            y_copy(k).wait_recv()
            value = (
                own[4 + k, 0:size]
                + cr[t, 4 + k, 0:size].astype(f32)
                + yr[t, k, 0:size].astype(f32)
            )

            @pl.when(k < Z - 1)
            def _():
                zs[k, 0:size] = value.astype(bf16)
                z_copy(k).start()

            @pl.when(k == Z - 1)
            def _():
                own[0, 0:size] = value

            return 0

        lax.fori_loop(0, Z, along, 0)
        if meanwhile is not None:
            meanwhile()

        def collect(k, total):
            z_copy(k).wait_recv()
            return total + zr[t, k, 0:size].astype(f32)

        total = lax.fori_loop(0, Z - 1, collect, own[0, 0:size])

        def drain(k, _):
            core_copy(k).wait_send()
            return 0

        lax.fori_loop(0, 8, drain, 0)

        def drain_y(k, _):
            y_copy(k).wait_send()
            return 0

        lax.fori_loop(0, 4, drain_y, 0)

        def drain_z(k, _):
            z_copy(k).wait_send()
            return 0

        lax.fori_loop(0, Z - 1, drain_z, 0)
        return total

    def squares_of(values):
        wide = values.astype(f32)
        column = jnp.sum(wide * wide, axis=1, keepdims=True)
        return jnp.broadcast_to(column_to_row(column), (8, rows))

    def inverse(total):
        return lax.rsqrt(total / D + 1e-05)

    squares_start(steps, sqe_ref[...])

    eye = (
        lax.broadcasted_iota(jnp.int32, (rows, rows), 0)
        == lax.broadcasted_iota(jnp.int32, (rows, rows), 1)
    ).astype(f32)

    depth = strip_ref.shape[0]

    def strip(n):
        second = n // 4 % 2
        zb = (z + 1 + n % 4) % Z
        yb = jnp.where(n < 8, 1 - y, y)
        cb = jnp.where(second == 0, 1 - c, c)
        at = pl.multiple_of((zb * 4 + yb * 2 + cb) * width, 128)
        return pltpu.make_async_copy(
            uniting_ref.at[:, pl.ds(at, width)], strip_ref.at[n % depth], strip_sem.at[n % depth]
        )

    weights = [
        pltpu.make_async_copy(src, dst, weight_sem.at[i])
        for i, (src, dst) in enumerate(
            ((we_hbm, we_ref), (wh_hbm, wh_ref), (wo_hbm, wo_ref))
        )
    ]

    def united_block(zb, yb, cb, dst, kind, n):
        strip(n).wait()
        dst[...] = jnp.dot(
            feats_ref[...], strip_ref[n % depth], preferred_element_type=f32
        ).astype(kind)

        @pl.when(n + depth < N)
        def _():
            strip(n + depth).start()

    def embed_products():
        for copy in weights:
            copy.wait()
        inve_ref[...] = inverse(squares_total(steps))
        columns = [row_to_column(eye, inve_ref[t : t + 1, :]) for t in range(steps + 1)]
        tall = jnp.concatenate(columns[:steps], axis=0)

        def go(i, _):
            at = pl.multiple_of(i * block_cols, 128)
            pe_ref[i] = (
                jnp.dot(
                    eg_ref[0 : steps * rows, :],
                    we_ref[:, pl.ds(at, block_cols)],
                    preferred_element_type=f32,
                )
                * tall
            )
            return 0

        lax.fori_loop(0, pe_ref.shape[0], go, 0)
        ctx_ref[...] = (
            jnp.dot(
                eg_ref[steps * rows : (steps + 1) * rows, :],
                we_ref[:, qcols:],
                preferred_element_type=f32,
            )
            * columns[steps]
        )

    for n in range(depth):
        strip(n).start()
    for copy in weights:
        copy.start()
    united = reduce_scatter(
        steps, 0, rows, united_block, uown_ref, ucs_ref, ucr_ref, uys_ref, uyr_ref, uzs_ref,
        uzr_ref, embed_products,
    ).astype(bf16)
    h_ref[...] = united
    squares_start(0, squares_of(united))

    def rope(values, cosine, sine):
        return values * cosine + pltpu.roll(values, HD // 2, 1) * sine

    def project(hg, at, size):
        return jnp.dot(hg, wh_ref[:, pl.ds(at, size)], preferred_element_type=f32)

    def kv_copy(slot, base, source, k):
        return remote(
            kv_ref.at[pl.ds(base + source * quarter, quarter)],
            kv_ref.at[pl.ds(base + source * quarter, quarter)],
            kvs_sem.at[slot, k],
            kvr_sem.at[slot, source],
            z * 4 + (yc + k) % 4,
        )

    def kv_put(slot, base, values, table):
        off = pl.multiple_of(yc * quarter, 8)
        cosine = cos_ref[table, pl.ds(off, quarter), :]
        sine = sin_ref[table, pl.ds(off, quarter), :]
        where = pl.ds(pl.multiple_of(base + yc * quarter, quarter), quarter)
        kv_ref[where, 0:HD] = rope(values[:, 0:HD], cosine, sine).astype(bf16)
        kv_ref[where, HD : 2 * HD] = values[:, HD : 2 * HD].astype(bf16)
        for k in range(1, 4):
            kv_copy(slot, base, yc, k).start()

    def kv_get(slot, base):
        for k in range(1, 4):
            kv_copy(slot, base, (yc + k) % 4, k).wait_recv()
            kv_copy(slot, base, yc, k).wait_send()

    def gather_copy(t, k, source, peer):
        return remote(
            att_ref.at[t, source], att_ref.at[t, source], ags_sem.at[t, k],
            agr_sem.at[t, source], peer,
        )

    def step(t, first):
        pick = pick_ref[t]
        h_in = jnp.dot(pick, h_ref[...], preferred_element_type=f32).astype(bf16)
        gain = gh_ref[0:1, :].astype(f32)
        hg = (h_in.astype(f32) * gain).astype(bf16)
        hg_ref[...] = hg
        inv = inverse(squares_total(t))[0:1]
        inv_h = row_to_column(pick, inv)
        own_rows = pl.ds(pl.multiple_of(t * rows, 128), rows)
        pairs = 2 * kcols // block_cols
        for i in range(pairs):
            at = i * block_cols
            kvp_ref[0, :, at : at + block_cols] = (
                pe_ref[N + i, own_rows] + project(hg, qcols + at, block_cols) * inv_h
            )
        if first:
            inv_u = row_to_column(eye, inv)
            ug = (h_ref[...].astype(f32) * gain).astype(bf16)
            for i in range(pairs):
                at = i * block_cols
                kvp_ref[1, :, at : at + block_cols] = (
                    ctx_ref[:, at : at + block_cols] + project(ug, qcols + at, block_cols) * inv_u
                )

        def block(zb, yb, cb, dst, kind, n):
            b = zb * 4 + yb * 2 + cb
            ph = project(hg_ref[...], pl.multiple_of(b * block_cols, 128), block_cols)
            dst[0:rows, :] = (pe_ref[b, own_rows] + ph * inv_h).astype(kind)
            off = pl.multiple_of((yb * 2 + cb) * quarter, 8)
            for which in range(2 if first else 1):
                for half in range(2):
                    at = pl.multiple_of(half * kcols + zb * HD, 128)
                    dst[
                        rows + which * quarter : rows + (which + 1) * quarter,
                        half * HD : (half + 1) * HD,
                    ] = kvp_ref[which, pl.ds(off, quarter), pl.ds(at, HD)].astype(kind)

        size = rows + (2 if first else 1) * quarter
        total = reduce_scatter(
            t, t, size, block, own_ref, cs_ref, cr_ref, ys_ref, yr_ref, zs_ref, zr_ref
        )
        sum_ref[0:size] = total
        base = rows + t * rows
        kv_put(t, base, sum_ref[rows : rows + quarter], t)
        if first:
            kv_put(steps, 0, sum_ref[rows + quarter : rows + 2 * quarter], steps)
        cosine, sine = cos_ref[t], sin_ref[t]
        queries = [
            rope(sum_ref[0:rows, j * HD : (j + 1) * HD], cosine, sine).astype(bf16)
            for j in range(block_cols // HD)
        ]
        kv_get(t, base)
        if first:
            kv_get(steps, 0)
        keys = kv_ref[:, 0:HD]
        vals = kv_ref[:, HD : 2 * HD]
        heads = len(queries)
        allowed = jnp.concatenate([mask_ref[t]] * heads, axis=0) > 0
        scores = lax.dot_general(
            jnp.concatenate(queries, axis=0),
            keys,
            (((1,), (1,)), ((), ())),
            preferred_element_type=f32,
        ) / math.sqrt(HD)
        scores = jnp.where(allowed, scores, MASKED)
        expo = jnp.exp(scores - jnp.max(scores, axis=1, keepdims=True))
        weights = (expo / jnp.sum(expo, axis=1, keepdims=True)).astype(bf16)
        mixed = jnp.dot(weights, vals, preferred_element_type=f32).astype(bf16)
        for j in range(heads):
            att_ref[t, me, :, j * HD : (j + 1) * HD] = mixed[j * rows : (j + 1) * rows]

        for k in range(1, Z):
            gather_copy(t, k, me, ((z + k) % Z) * 4 + yc).start()
        gather_copy(t, 4, me, y_peer).start()
        gather_copy(t, 8, me, sibling).start()

        def product(source):
            at = pl.multiple_of(source * block_cols, 128)
            return jnp.dot(
                att_ref[t, source], wo_ref[pl.ds(at, block_cols), :], preferred_element_type=f32
            )

        part_ref[...] = h_in.astype(f32) + product(me)
        for k in range(1, Z):
            source = ((z + k) % Z) * 4 + yc
            gather_copy(t, k, source, source).wait_recv()
            gather_copy(t, 4 + k, source, y_peer).start()
            gather_copy(t, 8 + k, source, sibling).start()
            part_ref[...] += product(source)
        for k in range(Z):
            source = ((z + k) % Z) * 4 + (1 - y) * 2 + c
            gather_copy(t, 4 + k, source, y_peer).wait_recv()
            gather_copy(t, 12 + k, source, sibling).start()
            part_ref[...] += product(source)
        for yk in range(2):
            for k in range(Z):
                source = ((z + k) % Z) * 4 + ((y + yk) % 2) * 2 + (1 - c)
                gather_copy(t, 8 + 4 * yk + k, source, sibling).wait_recv()
                part_ref[...] += product(source)
        for k in range(1, 16):
            gather_copy(t, k, me, sibling).wait_send()
        h_out = part_ref[...].astype(bf16)
        h_ref[...] = h_out
        hist_ref[t] = h_out
        for q in range(4):
            owner = t * 4 + q

            @pl.when(owner != me)
            def _():
                out_copy(t, q, me).start()

            @pl.when(owner == me)
            def _():
                rows_ref[me] = hist_ref[t, q * quarter : (q + 1) * quarter]

    def out_copy(t, q, source):
        return remote(
            hist_ref.at[t, pl.ds(q * quarter, quarter)],
            rows_ref.at[source],
            outs_sem.at[t, q],
            outr_sem.at[source],
            t * 4 + q,
        )

    step(0, True)

    def later(t, _):
        squares_start(t, squares_of(h_ref[...]))
        step(t, False)
        return 0

    lax.fori_loop(1, steps, later, 0)

    for t in range(steps):
        for q in range(4):

            @pl.when(t * 4 + q != me)
            def _():
                out_copy(t, q, me).wait_send()

    out_ref[:, pl.ds(pl.multiple_of(me * width, 128), width)] = rows_ref[me]

    def place(k, _):
        source = (me + k) % N
        out_copy(0, 0, source).wait_recv()
        out_ref[:, pl.ds(pl.multiple_of(source * width, 128), width)] = rows_ref[source]
        return 0

    lax.fori_loop(1, N, place, 0)


def local_kernel(
    feats,
    uniting_weight,
    embeds_verified,
    draft_embeds,
    gain_embed,
    gain_hidden,
    proj_embed,
    proj_hidden,
    out_proj,
    lengths,
    root_seq,
    parents,
):
    rows = feats.shape[0]
    steps = draft_embeds.shape[0]
    width = out_proj.shape[1]
    qcols = out_proj.shape[0]
    kcols = (proj_embed.shape[1] - qcols) // 2
    block_cols = qcols // N
    f32, bf16 = jnp.float32, jnp.bfloat16
    ends = jnp.cumsum(lengths)
    starts = ends - lengths
    ids = jnp.arange(rows, dtype=jnp.int32)
    slots = jnp.arange(lengths.shape[0], dtype=jnp.int32)
    seg = jnp.sum((ids[:, None] >= ends[None, :]).astype(jnp.int32), axis=1)
    of_seg = seg[:, None] == slots[None, :]
    pos_v = ids - jnp.sum(jnp.where(of_seg, starts[None, :], 0), axis=1)

    def look(table, index, count):
        hit = index[:, None] == jnp.arange(count, dtype=jnp.int32)[None, :]
        return jnp.sum(jnp.where(hit, table[None, :], 0), axis=1)

    seq = root_seq
    picks, masks, positions = [], [], []
    ancestors = []
    none = jnp.zeros((rows, rows), jnp.bool_)
    for t in range(steps):
        if t == 0:
            link = look(ends - 1, root_seq, lengths.shape[0])
        else:
            link = parents[t - 1]
            seq = look(seq, link, rows)
            ancestors = [look(older, link, rows) for older in ancestors] + [link]
        picks.append(link[:, None] == ids[None, :])
        positions.append(look(lengths, seq, lengths.shape[0]) + t)
        mask = [seg[None, :] == seq[:, None]]
        mask += [older[:, None] == ids[None, :] for older in ancestors]
        mask.append(ids[:, None] == ids[None, :])
        mask += [none] * (steps + 1 - len(mask))
        masks.append(jnp.concatenate(mask, axis=1))
    positions.append(pos_v)
    pick = jnp.stack(picks).astype(bf16)
    mask = jnp.stack(masks).astype(f32)
    half = HD // 2
    freq = 500000.0 ** (-(jnp.arange(half, dtype=f32) * 2.0 / HD))
    angle = jnp.stack(positions).astype(f32)[:, :, None] * freq[None, None, :]
    cosine, sine = jnp.cos(angle), jnp.sin(angle)
    cosine = jnp.concatenate([cosine, cosine], axis=-1)
    sine = jnp.concatenate([-sine, sine], axis=-1)
    embeds = jnp.concatenate([draft_embeds, embeds_verified[None]], axis=0)
    wide = embeds.astype(f32)
    eg = (wide * gain_embed.astype(f32)[None, None, :]).astype(bf16)
    eg = eg.reshape((steps + 1) * rows, width)
    sqe = jnp.sum(wide * wide, axis=-1)
    sqe = jnp.concatenate([sqe, jnp.zeros((8 - steps - 1, rows), f32)], axis=0)
    gh = jnp.broadcast_to(gain_hidden[None, :], (16, width))
    tall = rows + rows // 2
    vmem = pl.BlockSpec(memory_space=pltpu.VMEM)
    dma = pltpu.SemaphoreType.DMA
    hbm = pl.BlockSpec(memory_space=pl.ANY)
    return pl.pallas_call(
        functools.partial(draft_kernel, steps),
        out_shape=jax.ShapeDtypeStruct((steps * rows // N, N * width), bf16),
        in_specs=[vmem, hbm] + [vmem] * 3 + [hbm] * 3 + [vmem] * 4,
        out_specs=vmem,
        scratch_shapes=[
            pltpu.VMEM(proj_embed.shape, bf16),
            pltpu.VMEM(proj_hidden.shape, bf16),
            pltpu.VMEM(out_proj.shape, bf16),
            pltpu.VMEM((4, feats.shape[1], width), bf16),
            pltpu.VMEM((proj_embed.shape[1] // block_cols, steps * rows, block_cols), f32),
            pltpu.VMEM((rows, 2 * kcols), f32),
            pltpu.VMEM((steps, rows, width), bf16),
            pltpu.VMEM((N, rows // 4, width), bf16),
            dma((4,)),
            dma((3,)),
            dma((steps, 4)),
            dma((N,)),
            pltpu.VMEM((rows, width), bf16),
            pltpu.VMEM((rows, width), bf16),
            pltpu.VMEM((rows, width), f32),
            pltpu.VMEM((2, rows, 2 * kcols), f32),
            pltpu.VMEM((8, tall, block_cols), f32),
            pltpu.VMEM((8, tall, block_cols), bf16),
            pltpu.VMEM((steps, 8, tall, block_cols), bf16),
            pltpu.VMEM((4, tall, block_cols), bf16),
            pltpu.VMEM((steps, 4, tall, block_cols), bf16),
            pltpu.VMEM((4, tall, block_cols), bf16),
            pltpu.VMEM((steps, 4, tall, block_cols), bf16),
            pltpu.VMEM((8, rows, width), f32),
            pltpu.VMEM((8, rows, width), bf16),
            pltpu.VMEM((1, 8, rows, width), bf16),
            pltpu.VMEM((4, rows, width), bf16),
            pltpu.VMEM((1, 4, rows, width), bf16),
            pltpu.VMEM((4, rows, width), bf16),
            pltpu.VMEM((1, 4, rows, width), bf16),
            pltpu.VMEM((steps + 1, 8, rows), f32),
            pltpu.VMEM((steps + 1, N, 8, rows), f32),
            pltpu.VMEM(((steps + 1) * rows, 2 * HD), bf16),
            pltpu.VMEM((steps, N, rows, block_cols), bf16),
            pltpu.VMEM((tall, block_cols), f32),
            pltpu.VMEM((8, rows), f32),
            dma((steps + 1, 8)),
            dma((steps + 1, 8)),
            dma((steps + 1, 4)),
            dma((steps + 1, 4)),
            dma((steps + 1, 4)),
            dma((steps + 1, 4)),
            dma((steps + 1, N)),
            dma((steps + 1, N)),
            dma((steps + 1, 4)),
            dma((steps + 1, 4)),
            dma((steps, N)),
            dma((steps, N)),
        ],
        compiler_params=pltpu.CompilerParams(
            collective_id=0, has_side_effects=True, vmem_limit_bytes=60 * 1024 * 1024
        ),
    )(
        feats, uniting_weight, eg, sqe, gh, proj_embed, proj_hidden, out_proj, pick, mask, cosine,
        sine,
    )


def solution(mesh):
    return jax.shard_map(
        local_kernel if mesh.shape["section"] == N else local_plain,
        mesh=mesh,
        in_specs=(
            P("groups", "section"),
            P("section", None),
            P("groups", "section"),
            P(None, "groups", "section"),
            P("section"),
            P("section"),
            P("section", None),
            P("section", None),
            P(None, "section"),
            P("groups"),
            P("groups"),
            P(None, "groups"),
        ),
        out_specs=P(("groups", "section"), None),
        check_vma=False,
    )
```

```python
import functools
import math

import jax
import jax.numpy as jnp
from jax import lax
from jax.experimental import pallas as pl
from jax.experimental.pallas import tpu as pltpu
from jax.sharding import PartitionSpec as P

D = 8192
HD = 128


def rope_heads(values, positions):
    half = values.shape[-1] // 2
    freq = 500000.0 ** (-(jnp.arange(half, dtype=jnp.float32) * 2.0 / values.shape[-1]))
    angle = positions.astype(jnp.float32)[:, None] * freq[None, :]
    cosine = jnp.cos(angle)[:, None, :]
    sine = jnp.sin(angle)[:, None, :]
    first = values[..., :half]
    second = values[..., half:]
    return jnp.concatenate(
        [first * cosine - second * sine, second * cosine + first * sine], axis=-1
    )


def scaled_input(values, gain):
    return (values.astype(jnp.float32) * gain.astype(jnp.float32)[None, :]).astype(jnp.bfloat16)


def project_rows(embed_rows, hidden_rows, gain_embed, gain_hidden, w_embed, w_hidden):
    part_e = jnp.dot(
        scaled_input(embed_rows, gain_embed), w_embed, preferred_element_type=jnp.float32
    )
    part_h = jnp.dot(
        scaled_input(hidden_rows, gain_hidden), w_hidden, preferred_element_type=jnp.float32
    )
    square_e = jnp.sum(embed_rows.astype(jnp.float32) ** 2, axis=-1)
    square_h = jnp.sum(hidden_rows.astype(jnp.float32) ** 2, axis=-1)
    total_e, total_h = lax.psum((square_e, square_h), "section")
    inv_e = lax.rsqrt(total_e / D + 1e-05)
    inv_h = lax.rsqrt(total_h / D + 1e-05)
    return lax.psum(part_e * inv_e[:, None] + part_h * inv_h[:, None], "section")


def attend(queries, keys, values, allowed):
    nodes = queries.shape[0]
    kv_heads = keys.shape[1]
    group = queries.shape[1] // kv_heads
    grouped = queries.reshape(nodes, kv_heads, group, queries.shape[2])
    scores = jnp.einsum(
        "bkgd,nkd->bkgn", grouped, keys, preferred_element_type=jnp.float32
    ) / math.sqrt(queries.shape[2])
    scores = jnp.where(allowed[:, None, None, :], scores, -1e30)
    top = jnp.max(scores, axis=-1, keepdims=True)
    expo = jnp.exp(scores - top)
    weights = (expo / jnp.sum(expo, axis=-1, keepdims=True)).astype(jnp.bfloat16)
    mixed = jnp.einsum("bkgn,nkd->bkgd", weights, values, preferred_element_type=jnp.float32)
    return mixed.astype(jnp.bfloat16).reshape(nodes, -1)


def local_plain(
    feats,
    uniting_weight,
    embeds_verified,
    draft_embeds,
    gain_embed,
    gain_hidden,
    proj_embed,
    proj_hidden,
    out_proj,
    lengths,
    root_seq,
    parents,
):
    row_count = feats.shape[0]
    node_count = draft_embeds.shape[1]
    step_count = draft_embeds.shape[0]
    qcols = out_proj.shape[0]
    kcols = (proj_embed.shape[1] - qcols) // 2
    q_heads = qcols // HD
    kv_heads = kcols // HD
    ends = jnp.cumsum(lengths)
    starts = ends - lengths
    row_ids = jnp.arange(row_count, dtype=jnp.int32)
    seg = jnp.sum((row_ids[:, None] >= ends[None, :]).astype(jnp.int32), axis=1)
    pos_v = row_ids - starts[seg]
    last = ends - 1
    partial_value = jnp.dot(feats, uniting_weight, preferred_element_type=jnp.float32)
    united = lax.psum_scatter(partial_value, "section", scatter_dimension=1, tiled=True).astype(
        jnp.bfloat16
    )
    context = project_rows(
        embeds_verified,
        united,
        gain_embed,
        gain_hidden,
        proj_embed[:, qcols:],
        proj_hidden[:, qcols:],
    )
    keys_v = rope_heads(context[:, :kcols].reshape(row_count, kv_heads, HD), pos_v).astype(
        jnp.bfloat16
    )
    vals_v = context[:, kcols:].reshape(row_count, kv_heads, HD).astype(jnp.bfloat16)
    node_ids = jnp.arange(node_count, dtype=jnp.int32)
    node_keys = []
    node_vals = []
    ancestors = []
    drafts = []
    seq = root_seq
    h_out = united
    for step in range(step_count):
        if step == 0:
            h_in = jnp.take(united, last[root_seq], axis=0)
        else:
            link = parents[step - 1]
            h_in = jnp.take(h_out, link, axis=0)
            seq = seq[link]
            ancestors = [older[link] for older in ancestors] + [link]
        positions = lengths[seq] + step
        proj = project_rows(
            draft_embeds[step], h_in, gain_embed, gain_hidden, proj_embed, proj_hidden
        )
        queries = rope_heads(proj[:, :qcols].reshape(node_count, q_heads, HD), positions).astype(
            jnp.bfloat16
        )
        node_keys.append(
            rope_heads(
                proj[:, qcols : qcols + kcols].reshape(node_count, kv_heads, HD), positions
            ).astype(jnp.bfloat16)
        )
        node_vals.append(
            proj[:, qcols + kcols :].reshape(node_count, kv_heads, HD).astype(jnp.bfloat16)
        )
        masks = [seg[None, :] == seq[:, None]]
        for older in ancestors:
            masks.append(older[:, None] == node_ids[None, :])
        masks.append(node_ids[:, None] == node_ids[None, :])
        allowed = jnp.concatenate(masks, axis=1)
        keys = jnp.concatenate([keys_v] + node_keys, axis=0)
        values = jnp.concatenate([vals_v] + node_vals, axis=0)
        mixed = attend(queries, keys, values, allowed)
        h_out = (
            h_in.astype(jnp.float32) + jnp.dot(mixed, out_proj, preferred_element_type=jnp.float32)
        ).astype(jnp.bfloat16)
        drafts.append(h_out)
    columns = jnp.concatenate(drafts, axis=0)
    return lax.all_to_all(columns, "section", split_axis=0, concat_axis=1, tiled=True)


Z, Y, C = 4, 2, 2
N = Z * Y * C
MASKED = -1e30


def remote(src, dst, send, recv, peer):
    return pltpu.make_async_remote_copy(
        src_ref=src,
        dst_ref=dst,
        send_sem=send,
        recv_sem=recv,
        device_id={"section": peer},
        device_id_type=pl.DeviceIdType.MESH,
    )


def column_to_row(column):
    rows = lax.broadcasted_iota(jnp.int32, (column.shape[0], column.shape[0]), 0)
    cols = lax.broadcasted_iota(jnp.int32, (column.shape[0], column.shape[0]), 1)
    return jnp.sum(jnp.where(rows == cols, column, 0.0), axis=0, keepdims=True)


def row_to_column(pick, row):
    return jnp.sum(jnp.where(pick > 0, row, 0.0), axis=1, keepdims=True)


def draft_kernel(
    steps,
    feats_ref,
    uniting_ref,
    eg_ref,
    sqe_ref,
    gh_ref,
    we_hbm,
    wh_hbm,
    wo_hbm,
    pick_ref,
    mask_ref,
    cos_ref,
    sin_ref,
    out_ref,
    we_ref,
    wh_ref,
    wo_ref,
    strip_ref,
    pe_ref,
    ph_ref,
    ctx_ref,
    hist_ref,
    rows_ref,
    strip_sem,
    weight_sem,
    outs_sem,
    outr_sem,
    h_ref,
    hg_ref,
    part_ref,
    kvp_ref,
    own_ref,
    cs_ref,
    cr_ref,
    ys_ref,
    yr_ref,
    zs_ref,
    zr_ref,
    uown_ref,
    ucs_ref,
    ucr_ref,
    uys_ref,
    uyr_ref,
    uzs_ref,
    uzr_ref,
    sqs_ref,
    sqr_ref,
    kv_ref,
    att_ref,
    sum_ref,
    inve_ref,
    cs_sem,
    cr_sem,
    ys_sem,
    yr_sem,
    zs_sem,
    zr_sem,
    sqs_sem,
    sqr_sem,
    kvs_sem,
    kvr_sem,
    ags_sem,
    agr_sem,
):
    rows, width = h_ref.shape
    me = lax.axis_index("section")
    z = me // 4
    y = (me // 2) % 2
    c = me % 2
    yc = me % 4
    sibling = z * 4 + y * 2 + (1 - c)
    y_peer = z * 4 + (1 - y) * 2 + c
    quarter = rows // 4
    qcols = wo_ref.shape[0]
    kcols = (we_ref.shape[1] - qcols) // 2
    block_cols = qcols // N
    f32, bf16 = jnp.float32, jnp.bfloat16

    kv_ref[...] = jnp.zeros_like(kv_ref)

    barrier = pltpu.get_barrier_semaphore()

    def greet(k, _):
        pl.semaphore_signal(
            barrier,
            inc=1,
            device_id={"section": (me + k) % N},
            device_id_type=pl.DeviceIdType.MESH,
        )
        return 0

    lax.fori_loop(1, N, greet, 0)
    pl.semaphore_wait(barrier, N - 1)

    def squares_copy(slot, k, peer, source):
        return remote(
            sqs_ref.at[slot],
            sqr_ref.at[slot, source],
            sqs_sem.at[slot, k],
            sqr_sem.at[slot, source],
            peer,
        )

    def squares_start(slot, value):
        sqs_ref[slot] = value
        sqr_ref[slot, me] = value

        def go(k, _):
            squares_copy(slot, k, (me + k) % N, me).start()
            return 0

        lax.fori_loop(1, N, go, 0)

    def squares_total(slot):
        def go(k, total):
            source = (me + k) % N
            copy = squares_copy(slot, k, source, source)
            copy.wait_recv()
            copy.wait_send()
            return total + sqr_ref[slot, source]

        return lax.fori_loop(1, N, go, sqr_ref[slot, me])

    def reduce_scatter(s, t, size, block, own, cs, cr, ys, yr, zs, zr, meanwhile=None):
        def order(k):
            far = k < 4
            return (z + 1 + jnp.where(far, k, k - 4)) % Z, jnp.where(far, 1 - y, y)

        def core_copy(k):
            return remote(
                cs.at[k, pl.ds(0, size)], cr.at[t, k, pl.ds(0, size)], cs_sem.at[s, k],
                cr_sem.at[s, k], sibling,
            )

        def y_copy(k):
            return remote(
                ys.at[k, pl.ds(0, size)], yr.at[t, k, pl.ds(0, size)], ys_sem.at[s, k],
                yr_sem.at[s, k], y_peer,
            )

        def z_copy(k):
            return remote(
                zs.at[k, pl.ds(0, size)], zr.at[t, k, pl.ds(0, size)], zs_sem.at[s, k],
                zr_sem.at[s, k], ((z + 1 + k) % Z) * 4 + yc,
            )

        def give(k, _):
            zb, yb = order(k)
            block(zb, yb, 1 - c, cs.at[k], bf16, k + jnp.where(k < 4, 0, 4))
            core_copy(k).start()
            return 0

        def keep(k, _):
            zb, yb = order(k)
            block(zb, yb, c, own.at[k], f32, k + jnp.where(k < 4, 4, 8))
            return 0

        def across(k, _):
            keep(k, 0)
            core_copy(k).wait_recv()
            ys[k, 0:size] = (own[k, 0:size] + cr[t, k, 0:size].astype(f32)).astype(bf16)
            y_copy(k).start()
            return 0

        lax.fori_loop(0, 4, give, 0)
        lax.fori_loop(0, 4, across, 0)
        lax.fori_loop(4, 8, give, 0)
        lax.fori_loop(4, 8, keep, 0)

        def along(k, _):
            core_copy(k + 4).wait_recv()
            y_copy(k).wait_recv()
            value = (
                own[4 + k, 0:size]
                + cr[t, 4 + k, 0:size].astype(f32)
                + yr[t, k, 0:size].astype(f32)
            )

            @pl.when(k < Z - 1)
            def _():
                zs[k, 0:size] = value.astype(bf16)
                z_copy(k).start()

            @pl.when(k == Z - 1)
            def _():
                own[0, 0:size] = value

            return 0

        lax.fori_loop(0, Z, along, 0)
        if meanwhile is not None:
            meanwhile()

        def collect(k, total):
            z_copy(k).wait_recv()
            return total + zr[t, k, 0:size].astype(f32)

        total = lax.fori_loop(0, Z - 1, collect, own[0, 0:size])

        def drain():
            def both(k, _):
                core_copy(k).wait_send()
                return 0

            def cross(k, _):
                y_copy(k).wait_send()
                return 0

            def deep(k, _):
                z_copy(k).wait_send()
                return 0

            lax.fori_loop(0, 8, both, 0)
            lax.fori_loop(0, 4, cross, 0)
            lax.fori_loop(0, Z - 1, deep, 0)

        return total, drain

    def squares_of(values):
        wide = values.astype(f32)
        column = jnp.sum(wide * wide, axis=1, keepdims=True)
        return jnp.broadcast_to(column_to_row(column), (8, rows))

    def inverse(total):
        return lax.rsqrt(total / D + 1e-05)

    squares_start(steps, sqe_ref[...])

    eye = (
        lax.broadcasted_iota(jnp.int32, (rows, rows), 0)
        == lax.broadcasted_iota(jnp.int32, (rows, rows), 1)
    ).astype(f32)

    depth = strip_ref.shape[0]

    def strip(n):
        second = n // 4 % 2
        zb = (z + 1 + n % 4) % Z
        yb = jnp.where(n < 8, 1 - y, y)
        cb = jnp.where(second == 0, 1 - c, c)
        at = pl.multiple_of((zb * 4 + yb * 2 + cb) * width, 128)
        return pltpu.make_async_copy(
            uniting_ref.at[:, pl.ds(at, width)], strip_ref.at[n % depth], strip_sem.at[n % depth]
        )

    weights = [
        pltpu.make_async_copy(src, dst, weight_sem.at[i])
        for i, (src, dst) in enumerate(
            ((we_hbm, we_ref), (wh_hbm, wh_ref), (wo_hbm, wo_ref))
        )
    ]

    def united_block(zb, yb, cb, dst, kind, n):
        strip(n).wait()
        dst[...] = jnp.dot(
            feats_ref[...], strip_ref[n % depth], preferred_element_type=f32
        ).astype(kind)

        @pl.when(n + depth < N)
        def _():
            strip(n + depth).start()

    def embed_products():
        for copy in weights:
            copy.wait()
        inve_ref[...] = inverse(squares_total(steps))
        columns = [row_to_column(eye, inve_ref[t : t + 1, :]) for t in range(steps + 1)]
        tall = jnp.concatenate(columns[:steps], axis=0)

        def go(i, _):
            at = pl.multiple_of(i * block_cols, 128)
            pe_ref[i] = (
                jnp.dot(
                    eg_ref[0 : steps * rows, :],
                    we_ref[:, pl.ds(at, block_cols)],
                    preferred_element_type=f32,
                )
                * tall
            )
            return 0

        lax.fori_loop(0, pe_ref.shape[0], go, 0)
        ctx_ref[...] = (
            jnp.dot(
                eg_ref[steps * rows : (steps + 1) * rows, :],
                we_ref[:, qcols:],
                preferred_element_type=f32,
            )
            * columns[steps]
        )

    for n in range(depth):
        strip(n).start()
    for copy in weights:
        copy.start()
    united, drain_united = reduce_scatter(
        steps, 0, rows, united_block, uown_ref, ucs_ref, ucr_ref, uys_ref, uyr_ref, uzs_ref,
        uzr_ref, embed_products,
    )
    united = united.astype(bf16)
    h_ref[...] = united
    squares_start(0, squares_of(united))

    def rope(values, cosine, sine):
        return values * cosine + pltpu.roll(values, HD // 2, 1) * sine

    def project(hg, at, size):
        return jnp.dot(hg, wh_ref[:, pl.ds(at, size)], preferred_element_type=f32)

    def kv_copy(slot, base, source, k):
        return remote(
            kv_ref.at[pl.ds(base + source * quarter, quarter)],
            kv_ref.at[pl.ds(base + source * quarter, quarter)],
            kvs_sem.at[slot, k],
            kvr_sem.at[slot, source],
            z * 4 + (yc + k) % 4,
        )

    def kv_put(slot, base, values, table):
        off = pl.multiple_of(yc * quarter, 8)
        cosine = cos_ref[table, pl.ds(off, quarter), :]
        sine = sin_ref[table, pl.ds(off, quarter), :]
        where = pl.ds(pl.multiple_of(base + yc * quarter, quarter), quarter)
        kv_ref[where, 0:HD] = rope(values[:, 0:HD], cosine, sine).astype(bf16)
        kv_ref[where, HD : 2 * HD] = values[:, HD : 2 * HD].astype(bf16)
        for k in range(1, 4):
            kv_copy(slot, base, yc, k).start()

    def kv_get(slot, base):
        for k in range(1, 4):
            kv_copy(slot, base, (yc + k) % 4, k).wait_recv()
            kv_copy(slot, base, yc, k).wait_send()

    def gather_copy(t, k, source, peer):
        return remote(
            att_ref.at[t, source], att_ref.at[t, source], ags_sem.at[t, k],
            agr_sem.at[t, source], peer,
        )

    def step(t, first):
        pick = pick_ref[t]
        h_in = jnp.dot(pick, h_ref[...], preferred_element_type=f32).astype(bf16)
        gain = gh_ref[0:1, :].astype(f32)
        hg = (h_in.astype(f32) * gain).astype(bf16)
        hg_ref[...] = hg
        pairs = 2 * kcols // block_cols

        def raw(i, _):
            ph_ref[i] = project(hg_ref[...], pl.multiple_of(i * block_cols, 128), block_cols)
            return 0

        lax.fori_loop(0, N + pairs, raw, 0, unroll=4)
        if first:
            ug = (h_ref[...].astype(f32) * gain).astype(bf16)
            kvp_ref[1] = project(ug, qcols, 2 * kcols)
        inv = inverse(squares_total(t))[0:1]
        inv_h = row_to_column(pick, inv)
        own_rows = pl.ds(pl.multiple_of(t * rows, 128), rows)
        for i in range(pairs):
            at = i * block_cols
            kvp_ref[0, :, at : at + block_cols] = pe_ref[N + i, own_rows] + ph_ref[N + i] * inv_h
        if first:
            kvp_ref[1] = ctx_ref[...] + kvp_ref[1] * row_to_column(eye, inv)

        def block(zb, yb, cb, dst, kind, n):
            b = zb * 4 + yb * 2 + cb
            dst[0:rows, :] = (pe_ref[b, own_rows] + ph_ref[b] * inv_h).astype(kind)
            off = pl.multiple_of((yb * 2 + cb) * quarter, 8)
            for which in range(2 if first else 1):
                for half in range(2):
                    at = pl.multiple_of(half * kcols + zb * HD, 128)
                    dst[
                        rows + which * quarter : rows + (which + 1) * quarter,
                        half * HD : (half + 1) * HD,
                    ] = kvp_ref[which, pl.ds(off, quarter), pl.ds(at, HD)].astype(kind)

        size = rows + (2 if first else 1) * quarter
        total, drain = reduce_scatter(
            t, t, size, block, own_ref, cs_ref, cr_ref, ys_ref, yr_ref, zs_ref, zr_ref
        )
        sum_ref[0:size] = total
        base = rows + t * rows
        kv_put(t, base, sum_ref[rows : rows + quarter], t)
        if first:
            kv_put(steps, 0, sum_ref[rows + quarter : rows + 2 * quarter], steps)
        cosine, sine = cos_ref[t], sin_ref[t]
        queries = [
            rope(sum_ref[0:rows, j * HD : (j + 1) * HD], cosine, sine).astype(bf16)
            for j in range(block_cols // HD)
        ]
        kv_get(t, base)
        if first:
            kv_get(steps, 0)
        keys = kv_ref[:, 0:HD]
        vals = kv_ref[:, HD : 2 * HD]
        heads = len(queries)
        allowed = jnp.concatenate([mask_ref[t]] * heads, axis=0) > 0
        scores = lax.dot_general(
            jnp.concatenate(queries, axis=0),
            keys,
            (((1,), (1,)), ((), ())),
            preferred_element_type=f32,
        ) / math.sqrt(HD)
        scores = jnp.where(allowed, scores, MASKED)
        expo = jnp.exp(scores - jnp.max(scores, axis=1, keepdims=True))
        weights = (expo / jnp.sum(expo, axis=1, keepdims=True)).astype(bf16)
        mixed = jnp.dot(weights, vals, preferred_element_type=f32).astype(bf16)
        for j in range(heads):
            att_ref[t, me, :, j * HD : (j + 1) * HD] = mixed[j * rows : (j + 1) * rows]

        for k in range(1, Z):
            gather_copy(t, k, me, ((z + k) % Z) * 4 + yc).start()
        gather_copy(t, 4, me, y_peer).start()
        gather_copy(t, 8, me, sibling).start()

        def product(source):
            at = pl.multiple_of(source * block_cols, 128)
            return jnp.dot(
                att_ref[t, source], wo_ref[pl.ds(at, block_cols), :], preferred_element_type=f32
            )

        part_ref[...] = h_in.astype(f32) + product(me)
        for k in range(1, Z):
            source = ((z + k) % Z) * 4 + yc
            gather_copy(t, k, source, source).wait_recv()
            gather_copy(t, 4 + k, source, y_peer).start()
            gather_copy(t, 8 + k, source, sibling).start()
            part_ref[...] += product(source)
        for k in range(Z):
            source = ((z + k) % Z) * 4 + (1 - y) * 2 + c
            gather_copy(t, 4 + k, source, y_peer).wait_recv()
            gather_copy(t, 12 + k, source, sibling).start()
            part_ref[...] += product(source)
        for yk in range(2):
            for k in range(Z):
                source = ((z + k) % Z) * 4 + ((y + yk) % 2) * 2 + (1 - c)
                gather_copy(t, 8 + 4 * yk + k, source, sibling).wait_recv()
                part_ref[...] += product(source)
        h_out = part_ref[...].astype(bf16)
        h_ref[...] = h_out
        if first:
            squares_start(1, squares_of(h_out))
        else:

            @pl.when(t < steps - 1)
            def _():
                squares_start(t + 1, squares_of(h_ref[...]))

        hist_ref[t] = h_out
        for q in range(4):
            owner = t * 4 + q

            @pl.when(owner != me)
            def _():
                out_copy(t, q, me).start()

            @pl.when(owner == me)
            def _():
                rows_ref[me] = hist_ref[t, q * quarter : (q + 1) * quarter]

        drain()
        for k in range(1, 16):
            gather_copy(t, k, me, sibling).wait_send()
        if first:
            drain_united()

    def out_copy(t, q, source):
        return remote(
            hist_ref.at[t, pl.ds(q * quarter, quarter)],
            rows_ref.at[source],
            outs_sem.at[t, q],
            outr_sem.at[source],
            t * 4 + q,
        )

    step(0, True)

    def later(t, _):
        step(t, False)
        return 0

    lax.fori_loop(1, steps, later, 0)

    for t in range(steps):
        for q in range(4):

            @pl.when(t * 4 + q != me)
            def _():
                out_copy(t, q, me).wait_send()

    out_ref[:, pl.ds(pl.multiple_of(me * width, 128), width)] = rows_ref[me]

    def place(k, _):
        source = (me + k) % N
        out_copy(0, 0, source).wait_recv()
        out_ref[:, pl.ds(pl.multiple_of(source * width, 128), width)] = rows_ref[source]
        return 0

    lax.fori_loop(1, N, place, 0)


def local_kernel(
    feats,
    uniting_weight,
    embeds_verified,
    draft_embeds,
    gain_embed,
    gain_hidden,
    proj_embed,
    proj_hidden,
    out_proj,
    lengths,
    root_seq,
    parents,
):
    rows = feats.shape[0]
    steps = draft_embeds.shape[0]
    width = out_proj.shape[1]
    qcols = out_proj.shape[0]
    kcols = (proj_embed.shape[1] - qcols) // 2
    block_cols = qcols // N
    f32, bf16 = jnp.float32, jnp.bfloat16
    ends = jnp.cumsum(lengths)
    starts = ends - lengths
    ids = jnp.arange(rows, dtype=jnp.int32)
    slots = jnp.arange(lengths.shape[0], dtype=jnp.int32)
    seg = jnp.sum((ids[:, None] >= ends[None, :]).astype(jnp.int32), axis=1)
    of_seg = seg[:, None] == slots[None, :]
    pos_v = ids - jnp.sum(jnp.where(of_seg, starts[None, :], 0), axis=1)

    def look(table, index, count):
        hit = index[:, None] == jnp.arange(count, dtype=jnp.int32)[None, :]
        return jnp.sum(jnp.where(hit, table[None, :], 0), axis=1)

    seq = root_seq
    picks, masks, positions = [], [], []
    ancestors = []
    none = jnp.zeros((rows, rows), jnp.bool_)
    for t in range(steps):
        if t == 0:
            link = look(ends - 1, root_seq, lengths.shape[0])
        else:
            link = parents[t - 1]
            seq = look(seq, link, rows)
            ancestors = [look(older, link, rows) for older in ancestors] + [link]
        picks.append(link[:, None] == ids[None, :])
        positions.append(look(lengths, seq, lengths.shape[0]) + t)
        mask = [seg[None, :] == seq[:, None]]
        mask += [older[:, None] == ids[None, :] for older in ancestors]
        mask.append(ids[:, None] == ids[None, :])
        mask += [none] * (steps + 1 - len(mask))
        masks.append(jnp.concatenate(mask, axis=1))
    positions.append(pos_v)
    pick = jnp.stack(picks).astype(bf16)
    mask = jnp.stack(masks).astype(f32)
    half = HD // 2
    freq = 500000.0 ** (-(jnp.arange(half, dtype=f32) * 2.0 / HD))
    angle = jnp.stack(positions).astype(f32)[:, :, None] * freq[None, None, :]
    cosine, sine = jnp.cos(angle), jnp.sin(angle)
    cosine = jnp.concatenate([cosine, cosine], axis=-1)
    sine = jnp.concatenate([-sine, sine], axis=-1)
    embeds = jnp.concatenate([draft_embeds, embeds_verified[None]], axis=0)
    wide = embeds.astype(f32)
    eg = (wide * gain_embed.astype(f32)[None, None, :]).astype(bf16)
    eg = eg.reshape((steps + 1) * rows, width)
    sqe = jnp.sum(wide * wide, axis=-1)
    sqe = jnp.concatenate([sqe, jnp.zeros((8 - steps - 1, rows), f32)], axis=0)
    gh = jnp.broadcast_to(gain_hidden[None, :], (16, width))
    tall = rows + rows // 2
    vmem = pl.BlockSpec(memory_space=pltpu.VMEM)
    dma = pltpu.SemaphoreType.DMA
    hbm = pl.BlockSpec(memory_space=pl.ANY)
    return pl.pallas_call(
        functools.partial(draft_kernel, steps),
        out_shape=jax.ShapeDtypeStruct((steps * rows // N, N * width), bf16),
        in_specs=[vmem, hbm] + [vmem] * 3 + [hbm] * 3 + [vmem] * 4,
        out_specs=vmem,
        scratch_shapes=[
            pltpu.VMEM(proj_embed.shape, bf16),
            pltpu.VMEM(proj_hidden.shape, bf16),
            pltpu.VMEM(out_proj.shape, bf16),
            pltpu.VMEM((3, feats.shape[1], width), bf16),
            pltpu.VMEM((proj_embed.shape[1] // block_cols, steps * rows, block_cols), f32),
            pltpu.VMEM((proj_embed.shape[1] // block_cols, rows, block_cols), f32),
            pltpu.VMEM((rows, 2 * kcols), f32),
            pltpu.VMEM((steps, rows, width), bf16),
            pltpu.VMEM((N, rows // 4, width), bf16),
            dma((3,)),
            dma((3,)),
            dma((steps, 4)),
            dma((N,)),
            pltpu.VMEM((rows, width), bf16),
            pltpu.VMEM((rows, width), bf16),
            pltpu.VMEM((rows, width), f32),
            pltpu.VMEM((2, rows, 2 * kcols), f32),
            pltpu.VMEM((8, tall, block_cols), f32),
            pltpu.VMEM((8, tall, block_cols), bf16),
            pltpu.VMEM((steps, 8, tall, block_cols), bf16),
            pltpu.VMEM((4, tall, block_cols), bf16),
            pltpu.VMEM((steps, 4, tall, block_cols), bf16),
            pltpu.VMEM((4, tall, block_cols), bf16),
            pltpu.VMEM((steps, 4, tall, block_cols), bf16),
            pltpu.VMEM((8, rows, width), f32),
            pltpu.VMEM((8, rows, width), bf16),
            pltpu.VMEM((1, 8, rows, width), bf16),
            pltpu.VMEM((4, rows, width), bf16),
            pltpu.VMEM((1, 4, rows, width), bf16),
            pltpu.VMEM((4, rows, width), bf16),
            pltpu.VMEM((1, 4, rows, width), bf16),
            pltpu.VMEM((steps + 1, 8, rows), f32),
            pltpu.VMEM((steps + 1, N, 8, rows), f32),
            pltpu.VMEM(((steps + 1) * rows, 2 * HD), bf16),
            pltpu.VMEM((steps, N, rows, block_cols), bf16),
            pltpu.VMEM((tall, block_cols), f32),
            pltpu.VMEM((8, rows), f32),
            dma((steps + 1, 8)),
            dma((steps + 1, 8)),
            dma((steps + 1, 4)),
            dma((steps + 1, 4)),
            dma((steps + 1, 4)),
            dma((steps + 1, 4)),
            dma((steps + 1, N)),
            dma((steps + 1, N)),
            dma((steps + 1, 4)),
            dma((steps + 1, 4)),
            dma((steps, N)),
            dma((steps, N)),
        ],
        compiler_params=pltpu.CompilerParams(
            collective_id=0, has_side_effects=True, vmem_limit_bytes=60 * 1024 * 1024
        ),
    )(
        feats, uniting_weight, eg, sqe, gh, proj_embed, proj_hidden, out_proj, pick, mask, cosine,
        sine,
    )


def solution(mesh):
    return jax.shard_map(
        local_kernel if mesh.shape["section"] == N else local_plain,
        mesh=mesh,
        in_specs=(
            P("groups", "section"),
            P("section", None),
            P("groups", "section"),
            P(None, "groups", "section"),
            P("section"),
            P("section"),
            P("section", None),
            P("section", None),
            P(None, "section"),
            P("groups"),
            P("groups"),
            P(None, "groups"),
        ),
        out_specs=P(("groups", "section"), None),
        check_vma=False,
    )
```

```python
import functools
import math

import jax
import jax.numpy as jnp
from jax import lax
from jax.experimental import pallas as pl
from jax.experimental.pallas import tpu as pltpu
from jax.sharding import PartitionSpec as P

D = 8192
HD = 128


def rope_heads(values, positions):
    half = values.shape[-1] // 2
    freq = 500000.0 ** (-(jnp.arange(half, dtype=jnp.float32) * 2.0 / values.shape[-1]))
    angle = positions.astype(jnp.float32)[:, None] * freq[None, :]
    cosine = jnp.cos(angle)[:, None, :]
    sine = jnp.sin(angle)[:, None, :]
    first = values[..., :half]
    second = values[..., half:]
    return jnp.concatenate(
        [first * cosine - second * sine, second * cosine + first * sine], axis=-1
    )


def scaled_input(values, gain):
    return (values.astype(jnp.float32) * gain.astype(jnp.float32)[None, :]).astype(jnp.bfloat16)


def project_rows(embed_rows, hidden_rows, gain_embed, gain_hidden, w_embed, w_hidden):
    part_e = jnp.dot(
        scaled_input(embed_rows, gain_embed), w_embed, preferred_element_type=jnp.float32
    )
    part_h = jnp.dot(
        scaled_input(hidden_rows, gain_hidden), w_hidden, preferred_element_type=jnp.float32
    )
    square_e = jnp.sum(embed_rows.astype(jnp.float32) ** 2, axis=-1)
    square_h = jnp.sum(hidden_rows.astype(jnp.float32) ** 2, axis=-1)
    total_e, total_h = lax.psum((square_e, square_h), "section")
    inv_e = lax.rsqrt(total_e / D + 1e-05)
    inv_h = lax.rsqrt(total_h / D + 1e-05)
    return lax.psum(part_e * inv_e[:, None] + part_h * inv_h[:, None], "section")


def attend(queries, keys, values, allowed):
    nodes = queries.shape[0]
    kv_heads = keys.shape[1]
    group = queries.shape[1] // kv_heads
    grouped = queries.reshape(nodes, kv_heads, group, queries.shape[2])
    scores = jnp.einsum(
        "bkgd,nkd->bkgn", grouped, keys, preferred_element_type=jnp.float32
    ) / math.sqrt(queries.shape[2])
    scores = jnp.where(allowed[:, None, None, :], scores, -1e30)
    top = jnp.max(scores, axis=-1, keepdims=True)
    expo = jnp.exp(scores - top)
    weights = (expo / jnp.sum(expo, axis=-1, keepdims=True)).astype(jnp.bfloat16)
    mixed = jnp.einsum("bkgn,nkd->bkgd", weights, values, preferred_element_type=jnp.float32)
    return mixed.astype(jnp.bfloat16).reshape(nodes, -1)


def local_plain(
    feats,
    uniting_weight,
    embeds_verified,
    draft_embeds,
    gain_embed,
    gain_hidden,
    proj_embed,
    proj_hidden,
    out_proj,
    lengths,
    root_seq,
    parents,
):
    row_count = feats.shape[0]
    node_count = draft_embeds.shape[1]
    step_count = draft_embeds.shape[0]
    qcols = out_proj.shape[0]
    kcols = (proj_embed.shape[1] - qcols) // 2
    q_heads = qcols // HD
    kv_heads = kcols // HD
    ends = jnp.cumsum(lengths)
    starts = ends - lengths
    row_ids = jnp.arange(row_count, dtype=jnp.int32)
    seg = jnp.sum((row_ids[:, None] >= ends[None, :]).astype(jnp.int32), axis=1)
    pos_v = row_ids - starts[seg]
    last = ends - 1
    partial_value = jnp.dot(feats, uniting_weight, preferred_element_type=jnp.float32)
    united = lax.psum_scatter(partial_value, "section", scatter_dimension=1, tiled=True).astype(
        jnp.bfloat16
    )
    context = project_rows(
        embeds_verified,
        united,
        gain_embed,
        gain_hidden,
        proj_embed[:, qcols:],
        proj_hidden[:, qcols:],
    )
    keys_v = rope_heads(context[:, :kcols].reshape(row_count, kv_heads, HD), pos_v).astype(
        jnp.bfloat16
    )
    vals_v = context[:, kcols:].reshape(row_count, kv_heads, HD).astype(jnp.bfloat16)
    node_ids = jnp.arange(node_count, dtype=jnp.int32)
    node_keys = []
    node_vals = []
    ancestors = []
    drafts = []
    seq = root_seq
    h_out = united
    for step in range(step_count):
        if step == 0:
            h_in = jnp.take(united, last[root_seq], axis=0)
        else:
            link = parents[step - 1]
            h_in = jnp.take(h_out, link, axis=0)
            seq = seq[link]
            ancestors = [older[link] for older in ancestors] + [link]
        positions = lengths[seq] + step
        proj = project_rows(
            draft_embeds[step], h_in, gain_embed, gain_hidden, proj_embed, proj_hidden
        )
        queries = rope_heads(proj[:, :qcols].reshape(node_count, q_heads, HD), positions).astype(
            jnp.bfloat16
        )
        node_keys.append(
            rope_heads(
                proj[:, qcols : qcols + kcols].reshape(node_count, kv_heads, HD), positions
            ).astype(jnp.bfloat16)
        )
        node_vals.append(
            proj[:, qcols + kcols :].reshape(node_count, kv_heads, HD).astype(jnp.bfloat16)
        )
        masks = [seg[None, :] == seq[:, None]]
        for older in ancestors:
            masks.append(older[:, None] == node_ids[None, :])
        masks.append(node_ids[:, None] == node_ids[None, :])
        allowed = jnp.concatenate(masks, axis=1)
        keys = jnp.concatenate([keys_v] + node_keys, axis=0)
        values = jnp.concatenate([vals_v] + node_vals, axis=0)
        mixed = attend(queries, keys, values, allowed)
        h_out = (
            h_in.astype(jnp.float32) + jnp.dot(mixed, out_proj, preferred_element_type=jnp.float32)
        ).astype(jnp.bfloat16)
        drafts.append(h_out)
    columns = jnp.concatenate(drafts, axis=0)
    return lax.all_to_all(columns, "section", split_axis=0, concat_axis=1, tiled=True)


Z, Y, C = 4, 2, 2
N = Z * Y * C
MASKED = -1e30


def remote(src, dst, send, recv, peer):
    return pltpu.make_async_remote_copy(
        src_ref=src,
        dst_ref=dst,
        send_sem=send,
        recv_sem=recv,
        device_id={"section": peer},
        device_id_type=pl.DeviceIdType.MESH,
    )


def column_to_row(column):
    rows = lax.broadcasted_iota(jnp.int32, (column.shape[0], column.shape[0]), 0)
    cols = lax.broadcasted_iota(jnp.int32, (column.shape[0], column.shape[0]), 1)
    return jnp.sum(jnp.where(rows == cols, column, 0.0), axis=0, keepdims=True)


def row_to_column(pick, row):
    return jnp.sum(jnp.where(pick > 0, row, 0.0), axis=1, keepdims=True)


def draft_kernel(
    steps,
    feats_ref,
    uniting_ref,
    eg_ref,
    sqe_ref,
    gh_ref,
    we_hbm,
    wh_hbm,
    wo_hbm,
    pick_ref,
    mask_ref,
    cos_ref,
    sin_ref,
    out_ref,
    we_ref,
    wh_ref,
    wo_ref,
    strip_ref,
    pe_ref,
    ph_ref,
    ctx_ref,
    hist_ref,
    rows_ref,
    strip_sem,
    weight_sem,
    outs_sem,
    outr_sem,
    h_ref,
    hg_ref,
    part_ref,
    kvp_ref,
    own_ref,
    cs_ref,
    cr_ref,
    ys_ref,
    yr_ref,
    zs_ref,
    zr_ref,
    uown_ref,
    ucs_ref,
    ucr_ref,
    uys_ref,
    uyr_ref,
    uzs_ref,
    uzr_ref,
    sqs_ref,
    sqr_ref,
    kv_ref,
    att_ref,
    sum_ref,
    inve_ref,
    cs_sem,
    cr_sem,
    ys_sem,
    yr_sem,
    zs_sem,
    zr_sem,
    sqs_sem,
    sqr_sem,
    kvs_sem,
    kvr_sem,
    ags_sem,
    agr_sem,
):
    rows, width = h_ref.shape
    me = lax.axis_index("section")
    z = me // 4
    y = (me // 2) % 2
    c = me % 2
    yc = me % 4
    sibling = z * 4 + y * 2 + (1 - c)
    y_peer = z * 4 + (1 - y) * 2 + c
    quarter = rows // 4
    qcols = wo_ref.shape[0]
    kcols = (we_ref.shape[1] - qcols) // 2
    block_cols = qcols // N
    f32, bf16 = jnp.float32, jnp.bfloat16

    kv_ref[...] = jnp.zeros_like(kv_ref)

    barrier = pltpu.get_barrier_semaphore()

    def greet(k, _):
        pl.semaphore_signal(
            barrier,
            inc=1,
            device_id={"section": (me + k) % N},
            device_id_type=pl.DeviceIdType.MESH,
        )
        return 0

    lax.fori_loop(1, N, greet, 0)
    pl.semaphore_wait(barrier, N - 1)

    def squares_copy(slot, k, peer, source):
        return remote(
            sqs_ref.at[slot],
            sqr_ref.at[slot, source],
            sqs_sem.at[slot, k],
            sqr_sem.at[slot, source],
            peer,
        )

    def squares_start(slot, value):
        sqs_ref[slot] = value
        sqr_ref[slot, me] = value

        def go(k, _):
            squares_copy(slot, k, (me + k) % N, me).start()
            return 0

        lax.fori_loop(1, N, go, 0)

    def squares_total(slot):
        def go(k, total):
            source = (me + k) % N
            copy = squares_copy(slot, k, source, source)
            copy.wait_recv()
            copy.wait_send()
            return total + sqr_ref[slot, source]

        return lax.fori_loop(1, N, go, sqr_ref[slot, me])

    def reduce_scatter(s, t, size, block, own, cs, cr, ys, yr, zs, zr, meanwhile=None):
        def order(k):
            far = k < 4
            return (z + 1 + jnp.where(far, k, k - 4)) % Z, jnp.where(far, 1 - y, y)

        def core_copy(k):
            return remote(
                cs.at[k, pl.ds(0, size)], cr.at[t, k, pl.ds(0, size)], cs_sem.at[s, k],
                cr_sem.at[s, k], sibling,
            )

        def y_copy(k):
            return remote(
                ys.at[k, pl.ds(0, size)], yr.at[t, k, pl.ds(0, size)], ys_sem.at[s, k],
                yr_sem.at[s, k], y_peer,
            )

        def z_copy(k):
            return remote(
                zs.at[k, pl.ds(0, size)], zr.at[t, k, pl.ds(0, size)], zs_sem.at[s, k],
                zr_sem.at[s, k], ((z + 1 + k) % Z) * 4 + yc,
            )

        def give(k, _):
            zb, yb = order(k)
            block(zb, yb, 1 - c, cs.at[k], bf16, k + jnp.where(k < 4, 0, 4))
            core_copy(k).start()
            return 0

        def keep(k, _):
            zb, yb = order(k)
            block(zb, yb, c, own.at[k], f32, k + jnp.where(k < 4, 4, 8))
            return 0

        def across(k, _):
            keep(k, 0)
            core_copy(k).wait_recv()
            ys[k, 0:size] = (own[k, 0:size] + cr[t, k, 0:size].astype(f32)).astype(bf16)
            y_copy(k).start()
            return 0

        lax.fori_loop(0, 4, give, 0)
        lax.fori_loop(0, 4, across, 0)
        lax.fori_loop(4, 8, give, 0)
        lax.fori_loop(4, 8, keep, 0)

        def along(k, _):
            core_copy(k + 4).wait_recv()
            y_copy(k).wait_recv()
            value = (
                own[4 + k, 0:size]
                + cr[t, 4 + k, 0:size].astype(f32)
                + yr[t, k, 0:size].astype(f32)
            )

            @pl.when(k < Z - 1)
            def _():
                zs[k, 0:size] = value.astype(bf16)
                z_copy(k).start()

            @pl.when(k == Z - 1)
            def _():
                own[0, 0:size] = value

            return 0

        lax.fori_loop(0, Z, along, 0)
        if meanwhile is not None:
            meanwhile()

        def collect(k, total):
            z_copy(k).wait_recv()
            return total + zr[t, k, 0:size].astype(f32)

        total = lax.fori_loop(0, Z - 1, collect, own[0, 0:size])

        def drain():
            def both(k, _):
                core_copy(k).wait_send()
                return 0

            def cross(k, _):
                y_copy(k).wait_send()
                return 0

            def deep(k, _):
                z_copy(k).wait_send()
                return 0

            lax.fori_loop(0, 8, both, 0)
            lax.fori_loop(0, 4, cross, 0)
            lax.fori_loop(0, Z - 1, deep, 0)

        return total, drain

    def squares_of(values):
        wide = values.astype(f32)
        column = jnp.sum(wide * wide, axis=1, keepdims=True)
        return jnp.broadcast_to(column_to_row(column), (8, rows))

    def inverse(total):
        return lax.rsqrt(total / D + 1e-05)

    squares_start(steps, sqe_ref[...])

    eye = (
        lax.broadcasted_iota(jnp.int32, (rows, rows), 0)
        == lax.broadcasted_iota(jnp.int32, (rows, rows), 1)
    ).astype(f32)

    depth = strip_ref.shape[0]

    def strip(n):
        second = n // 4 % 2
        zb = (z + 1 + n % 4) % Z
        yb = jnp.where(n < 8, 1 - y, y)
        cb = jnp.where(second == 0, 1 - c, c)
        at = pl.multiple_of((zb * 4 + yb * 2 + cb) * width, 128)
        return pltpu.make_async_copy(
            uniting_ref.at[:, pl.ds(at, width)], strip_ref.at[n % depth], strip_sem.at[n % depth]
        )

    weights = [
        pltpu.make_async_copy(src, dst, weight_sem.at[i])
        for i, (src, dst) in enumerate(
            ((we_hbm, we_ref), (wh_hbm, wh_ref), (wo_hbm, wo_ref))
        )
    ]

    def united_block(zb, yb, cb, dst, kind, n):
        strip(n).wait()
        dst[...] = jnp.dot(
            feats_ref[...], strip_ref[n % depth], preferred_element_type=f32
        ).astype(kind)

        @pl.when(n + depth < N)
        def _():
            strip(n + depth).start()

    def embed_products():
        for copy in weights:
            copy.wait()
        inve_ref[...] = inverse(squares_total(steps))
        columns = [row_to_column(eye, inve_ref[t : t + 1, :]) for t in range(steps + 1)]
        tall = jnp.concatenate(columns[:steps], axis=0)

        def go(i, _):
            at = pl.multiple_of(i * block_cols, 128)
            pe_ref[i] = (
                jnp.dot(
                    eg_ref[0 : steps * rows, :],
                    we_ref[:, pl.ds(at, block_cols)],
                    preferred_element_type=f32,
                )
                * tall
            )
            return 0

        lax.fori_loop(0, pe_ref.shape[0], go, 0)
        ctx_ref[...] = (
            jnp.dot(
                eg_ref[steps * rows : (steps + 1) * rows, :],
                we_ref[:, qcols:],
                preferred_element_type=f32,
            )
            * columns[steps]
        )

    for n in range(depth):
        strip(n).start()
    for copy in weights:
        copy.start()
    united, drain_united = reduce_scatter(
        steps, 0, rows, united_block, uown_ref, ucs_ref, ucr_ref, uys_ref, uyr_ref, uzs_ref,
        uzr_ref, embed_products,
    )
    united = united.astype(bf16)
    h_ref[...] = united
    squares_start(0, squares_of(united))

    def rope(values, cosine, sine):
        return values * cosine + pltpu.roll(values, HD // 2, 1) * sine

    def project(hg, at, size):
        return jnp.dot(hg, wh_ref[:, pl.ds(at, size)], preferred_element_type=f32)

    def kv_copy(slot, base, source, k):
        return remote(
            kv_ref.at[pl.ds(base + source * quarter, quarter)],
            kv_ref.at[pl.ds(base + source * quarter, quarter)],
            kvs_sem.at[slot, k],
            kvr_sem.at[slot, source],
            z * 4 + (yc + k) % 4,
        )

    def kv_put(slot, base, values, table):
        off = pl.multiple_of(yc * quarter, 8)
        cosine = cos_ref[table, pl.ds(off, quarter), :]
        sine = sin_ref[table, pl.ds(off, quarter), :]
        where = pl.ds(pl.multiple_of(base + yc * quarter, quarter), quarter)
        kv_ref[where, 0:HD] = rope(values[:, 0:HD], cosine, sine).astype(bf16)
        kv_ref[where, HD : 2 * HD] = values[:, HD : 2 * HD].astype(bf16)
        for k in range(1, 4):
            kv_copy(slot, base, yc, k).start()

    def kv_get(slot, base):
        for k in range(1, 4):
            kv_copy(slot, base, (yc + k) % 4, k).wait_recv()
            kv_copy(slot, base, yc, k).wait_send()

    def gather_copy(t, k, source, peer):
        return remote(
            att_ref.at[t, source], att_ref.at[t, source], ags_sem.at[t, k],
            agr_sem.at[t, source], peer,
        )

    def step(t, first):
        pick = pick_ref[t]
        h_in = jnp.dot(pick, h_ref[...], preferred_element_type=f32).astype(bf16)
        gain = gh_ref[0:1, :].astype(f32)
        hg = (h_in.astype(f32) * gain).astype(bf16)
        hg_ref[...] = hg
        pairs = 2 * kcols // block_cols

        def raw(i, _):
            ph_ref[i] = project(hg_ref[...], pl.multiple_of(i * block_cols, 128), block_cols)
            return 0

        lax.fori_loop(0, N + pairs, raw, 0, unroll=4)
        if first:
            ug = (h_ref[...].astype(f32) * gain).astype(bf16)
            kvp_ref[1] = project(ug, qcols, 2 * kcols)
        inv = inverse(squares_total(t))[0:1]
        inv_h = row_to_column(pick, inv)
        own_rows = pl.ds(pl.multiple_of(t * rows, 128), rows)
        for i in range(pairs):
            at = i * block_cols
            kvp_ref[0, :, at : at + block_cols] = pe_ref[N + i, own_rows] + ph_ref[N + i] * inv_h
        if first:
            kvp_ref[1] = ctx_ref[...] + kvp_ref[1] * row_to_column(eye, inv)

        def block(zb, yb, cb, dst, kind, n):
            b = zb * 4 + yb * 2 + cb
            dst[0:rows, :] = (pe_ref[b, own_rows] + ph_ref[b] * inv_h).astype(kind)
            off = pl.multiple_of((yb * 2 + cb) * quarter, 8)
            for which in range(2 if first else 1):
                for half in range(2):
                    at = pl.multiple_of(half * kcols + zb * HD, 128)
                    dst[
                        rows + which * quarter : rows + (which + 1) * quarter,
                        half * HD : (half + 1) * HD,
                    ] = kvp_ref[which, pl.ds(off, quarter), pl.ds(at, HD)].astype(kind)

        size = rows + (2 if first else 1) * quarter
        total, drain = reduce_scatter(
            t, t, size, block, own_ref, cs_ref, cr_ref, ys_ref, yr_ref, zs_ref, zr_ref
        )
        sum_ref[0:size] = total
        base = rows + t * rows
        kv_put(t, base, sum_ref[rows : rows + quarter], t)
        if first:
            kv_put(steps, 0, sum_ref[rows + quarter : rows + 2 * quarter], steps)
        cosine, sine = cos_ref[t], sin_ref[t]
        queries = [
            rope(sum_ref[0:rows, j * HD : (j + 1) * HD], cosine, sine).astype(bf16)
            for j in range(block_cols // HD)
        ]
        kv_get(t, base)
        if first:
            kv_get(steps, 0)
        span = 2 * rows if first else kv_ref.shape[0]
        keys = kv_ref[0:span, 0:HD]
        vals = kv_ref[0:span, HD : 2 * HD]
        heads = len(queries)
        allowed = jnp.concatenate([mask_ref[t, :, 0:span]] * heads, axis=0) > 0
        scores = lax.dot_general(
            jnp.concatenate(queries, axis=0),
            keys,
            (((1,), (1,)), ((), ())),
            preferred_element_type=f32,
        ) * (1.0 / math.sqrt(HD))
        scores = jnp.where(allowed, scores, MASKED)
        expo = jnp.exp(scores - jnp.max(scores, axis=1, keepdims=True))
        weights = (expo * (1.0 / jnp.sum(expo, axis=1, keepdims=True))).astype(bf16)
        mixed = jnp.dot(weights, vals, preferred_element_type=f32).astype(bf16)
        for j in range(heads):
            att_ref[t, me, :, j * HD : (j + 1) * HD] = mixed[j * rows : (j + 1) * rows]

        for k in range(1, Z):
            gather_copy(t, k, me, ((z + k) % Z) * 4 + yc).start()
        gather_copy(t, 4, me, y_peer).start()
        gather_copy(t, 8, me, sibling).start()

        def product(source):
            at = pl.multiple_of(source * block_cols, 128)
            return jnp.dot(
                att_ref[t, source], wo_ref[pl.ds(at, block_cols), :], preferred_element_type=f32
            )

        part_ref[...] = h_in.astype(f32) + product(me)
        for k in range(1, Z):
            source = ((z + k) % Z) * 4 + yc
            gather_copy(t, k, source, source).wait_recv()
            gather_copy(t, 4 + k, source, y_peer).start()
            gather_copy(t, 8 + k, source, sibling).start()
            part_ref[...] += product(source)
        for k in range(Z):
            source = ((z + k) % Z) * 4 + (1 - y) * 2 + c
            gather_copy(t, 4 + k, source, y_peer).wait_recv()
            gather_copy(t, 12 + k, source, sibling).start()
            part_ref[...] += product(source)
        for yk in range(2):
            for k in range(Z):
                source = ((z + k) % Z) * 4 + ((y + yk) % 2) * 2 + (1 - c)
                gather_copy(t, 8 + 4 * yk + k, source, sibling).wait_recv()
                part_ref[...] += product(source)
        h_out = part_ref[...].astype(bf16)
        h_ref[...] = h_out
        if first:
            squares_start(1, squares_of(h_out))
        else:

            @pl.when(t < steps - 1)
            def _():
                squares_start(t + 1, squares_of(h_ref[...]))

        hist_ref[t] = h_out
        for q in range(4):
            owner = t * 4 + q

            @pl.when(owner != me)
            def _():
                out_copy(t, q, me).start()

            @pl.when(owner == me)
            def _():
                rows_ref[me] = hist_ref[t, q * quarter : (q + 1) * quarter]

        drain()
        for k in range(1, 16):
            gather_copy(t, k, me, sibling).wait_send()
        if first:
            drain_united()

    def out_copy(t, q, source):
        return remote(
            hist_ref.at[t, pl.ds(q * quarter, quarter)],
            rows_ref.at[source],
            outs_sem.at[t, q],
            outr_sem.at[source],
            t * 4 + q,
        )

    step(0, True)

    def later(t, _):
        step(t, False)
        return 0

    lax.fori_loop(1, steps, later, 0)

    for t in range(steps):
        for q in range(4):

            @pl.when(t * 4 + q != me)
            def _():
                out_copy(t, q, me).wait_send()

    out_ref[:, pl.ds(pl.multiple_of(me * width, 128), width)] = rows_ref[me]

    def place(k, _):
        source = (me + k) % N
        out_copy(0, 0, source).wait_recv()
        out_ref[:, pl.ds(pl.multiple_of(source * width, 128), width)] = rows_ref[source]
        return 0

    lax.fori_loop(1, N, place, 0)


def local_kernel(
    feats,
    uniting_weight,
    embeds_verified,
    draft_embeds,
    gain_embed,
    gain_hidden,
    proj_embed,
    proj_hidden,
    out_proj,
    lengths,
    root_seq,
    parents,
):
    rows = feats.shape[0]
    steps = draft_embeds.shape[0]
    width = out_proj.shape[1]
    qcols = out_proj.shape[0]
    kcols = (proj_embed.shape[1] - qcols) // 2
    block_cols = qcols // N
    f32, bf16 = jnp.float32, jnp.bfloat16
    ends = jnp.cumsum(lengths)
    starts = ends - lengths
    ids = jnp.arange(rows, dtype=jnp.int32)
    slots = jnp.arange(lengths.shape[0], dtype=jnp.int32)
    seg = jnp.sum((ids[:, None] >= ends[None, :]).astype(jnp.int32), axis=1)
    of_seg = seg[:, None] == slots[None, :]
    pos_v = ids - jnp.sum(jnp.where(of_seg, starts[None, :], 0), axis=1)

    def look(table, index, count):
        hit = index[:, None] == jnp.arange(count, dtype=jnp.int32)[None, :]
        return jnp.sum(jnp.where(hit, table[None, :], 0), axis=1)

    seq = root_seq
    picks, masks, positions = [], [], []
    ancestors = []
    none = jnp.zeros((rows, rows), jnp.bool_)
    for t in range(steps):
        if t == 0:
            link = look(ends - 1, root_seq, lengths.shape[0])
        else:
            link = parents[t - 1]
            seq = look(seq, link, rows)
            ancestors = [look(older, link, rows) for older in ancestors] + [link]
        picks.append(link[:, None] == ids[None, :])
        positions.append(look(lengths, seq, lengths.shape[0]) + t)
        mask = [seg[None, :] == seq[:, None]]
        mask += [older[:, None] == ids[None, :] for older in ancestors]
        mask.append(ids[:, None] == ids[None, :])
        mask += [none] * (steps + 1 - len(mask))
        masks.append(jnp.concatenate(mask, axis=1))
    positions.append(pos_v)
    pick = jnp.stack(picks).astype(bf16)
    mask = jnp.stack(masks).astype(f32)
    half = HD // 2
    freq = 500000.0 ** (-(jnp.arange(half, dtype=f32) * 2.0 / HD))
    angle = jnp.stack(positions).astype(f32)[:, :, None] * freq[None, None, :]
    cosine, sine = jnp.cos(angle), jnp.sin(angle)
    cosine = jnp.concatenate([cosine, cosine], axis=-1)
    sine = jnp.concatenate([-sine, sine], axis=-1)
    embeds = jnp.concatenate([draft_embeds, embeds_verified[None]], axis=0)
    wide = embeds.astype(f32)
    eg = (wide * gain_embed.astype(f32)[None, None, :]).astype(bf16)
    eg = eg.reshape((steps + 1) * rows, width)
    sqe = jnp.sum(wide * wide, axis=-1)
    sqe = jnp.concatenate([sqe, jnp.zeros((8 - steps - 1, rows), f32)], axis=0)
    gh = jnp.broadcast_to(gain_hidden[None, :], (16, width))
    tall = rows + rows // 2
    vmem = pl.BlockSpec(memory_space=pltpu.VMEM)
    dma = pltpu.SemaphoreType.DMA
    hbm = pl.BlockSpec(memory_space=pl.ANY)
    return pl.pallas_call(
        functools.partial(draft_kernel, steps),
        out_shape=jax.ShapeDtypeStruct((steps * rows // N, N * width), bf16),
        in_specs=[vmem, hbm] + [vmem] * 3 + [hbm] * 3 + [vmem] * 4,
        out_specs=vmem,
        scratch_shapes=[
            pltpu.VMEM(proj_embed.shape, bf16),
            pltpu.VMEM(proj_hidden.shape, bf16),
            pltpu.VMEM(out_proj.shape, bf16),
            pltpu.VMEM((3, feats.shape[1], width), bf16),
            pltpu.VMEM((proj_embed.shape[1] // block_cols, steps * rows, block_cols), f32),
            pltpu.VMEM((proj_embed.shape[1] // block_cols, rows, block_cols), f32),
            pltpu.VMEM((rows, 2 * kcols), f32),
            pltpu.VMEM((steps, rows, width), bf16),
            pltpu.VMEM((N, rows // 4, width), bf16),
            dma((3,)),
            dma((3,)),
            dma((steps, 4)),
            dma((N,)),
            pltpu.VMEM((rows, width), bf16),
            pltpu.VMEM((rows, width), bf16),
            pltpu.VMEM((rows, width), f32),
            pltpu.VMEM((2, rows, 2 * kcols), f32),
            pltpu.VMEM((8, tall, block_cols), f32),
            pltpu.VMEM((8, tall, block_cols), bf16),
            pltpu.VMEM((steps, 8, tall, block_cols), bf16),
            pltpu.VMEM((4, tall, block_cols), bf16),
            pltpu.VMEM((steps, 4, tall, block_cols), bf16),
            pltpu.VMEM((4, tall, block_cols), bf16),
            pltpu.VMEM((steps, 4, tall, block_cols), bf16),
            pltpu.VMEM((8, rows, width), f32),
            pltpu.VMEM((8, rows, width), bf16),
            pltpu.VMEM((1, 8, rows, width), bf16),
            pltpu.VMEM((4, rows, width), bf16),
            pltpu.VMEM((1, 4, rows, width), bf16),
            pltpu.VMEM((4, rows, width), bf16),
            pltpu.VMEM((1, 4, rows, width), bf16),
            pltpu.VMEM((steps + 1, 8, rows), f32),
            pltpu.VMEM((steps + 1, N, 8, rows), f32),
            pltpu.VMEM(((steps + 1) * rows, 2 * HD), bf16),
            pltpu.VMEM((steps, N, rows, block_cols), bf16),
            pltpu.VMEM((tall, block_cols), f32),
            pltpu.VMEM((8, rows), f32),
            dma((steps + 1, 8)),
            dma((steps + 1, 8)),
            dma((steps + 1, 4)),
            dma((steps + 1, 4)),
            dma((steps + 1, 4)),
            dma((steps + 1, 4)),
            dma((steps + 1, N)),
            dma((steps + 1, N)),
            dma((steps + 1, 4)),
            dma((steps + 1, 4)),
            dma((steps, N)),
            dma((steps, N)),
        ],
        compiler_params=pltpu.CompilerParams(
            collective_id=0, has_side_effects=True, vmem_limit_bytes=60 * 1024 * 1024
        ),
    )(
        feats, uniting_weight, eg, sqe, gh, proj_embed, proj_hidden, out_proj, pick, mask, cosine,
        sine,
    )


def solution(mesh):
    return jax.shard_map(
        local_kernel if mesh.shape["section"] == N else local_plain,
        mesh=mesh,
        in_specs=(
            P("groups", "section"),
            P("section", None),
            P("groups", "section"),
            P(None, "groups", "section"),
            P("section"),
            P("section"),
            P("section", None),
            P("section", None),
            P(None, "section"),
            P("groups"),
            P("groups"),
            P(None, "groups"),
        ),
        out_specs=P(("groups", "section"), None),
        check_vma=False,
    )
```
